512 devices in a mesh: ctx: 128 (over z, x, core), tp: 4 (over y).
Axes of the slice: x: 4, y: 4, z: 16, core: 2. Of those that a mesh axis runs over, the one named last changes fastest.
Arguments:
- resid: bfloat16 [16384, 8192], P('ctx', 'tp'), may hold values from -64 to 64
- q_mr: bfloat16 [16384, 8192], P('ctx', 'tp'), may hold values from -4 to 4
- k_mr: bfloat16 [16384, 8192], P('ctx', 'tp'), may hold values from -4 to 4
- v_mr: bfloat16 [16384, 8192], P('ctx', 'tp'), may hold values from -4 to 4
- mr_taps: bfloat16 [512, 128], P('tp'), may hold values from -0.5 to 0.5
- norm_gain: bfloat16 [8192], P('tp'), may hold values from 0.099609375 to 1.8984375
- q_lr: bfloat16 [16384, 8192], P('ctx', 'tp'), may hold values from -4 to 4
- k_lr: bfloat16 [16384, 8192], P('ctx', 'tp'), may hold values from -4 to 4
- pole_rate: float32 [16, 512], P(None, 'tp'), may hold values from 0 to 1, as said below
- residue: float32 [16, 512], P(None, 'tp'), may hold values from -3 to 3
Outputs:
- mixed: bfloat16 [16384, 8192], P('ctx', 'tp')
- lr_out: bfloat16 [16384, 8192], P('ctx', 'tp')
The draws below stay inside these ranges and needn't reach their ends.
Inputs may be any that keep to these rules, and one draw needn't show every extreme that they name: `pole_rate`: every rate is positive.
All inputs are finite; a program needn't handle non-finite values.
Results may differ from the reference program's by a relative error of at most 0.0052.
Values may be sent and summed in bfloat16 or wider, within the bound.
A program may use at most 128 MiB of HBM per device.

```python
import jax
import jax.numpy as jnp
from jax import lax

D = 8192
GROUP = 16
POLES = 16
FILT = 128
TOK_DEV = 128
TOKENS = 16384
GROUPS = 512


def draw_resid(key, part):
    first_key, second_key = jax.random.split(key)
    column_pos = (jnp.arange(D, dtype=jnp.float32) + 0.5) / D
    base = jnp.clip(jax.random.normal(first_key, (TOKENS, D), jnp.float32), -4.0, 4.0)
    row_scale = jnp.exp(jax.random.uniform(second_key, (TOKENS, 1), jnp.float32, jnp.log(0.3), jnp.log(3.0)))
    col_scale = 3.0 ** column_pos
    return (base * row_scale * col_scale[None, :]).astype(jnp.bfloat16)


def draw_pole_rate(key, part):
    mask_key, slow_key, fast_key = jax.random.split(key, 3)
    share = 0.5
    slow_mask = jax.random.uniform(mask_key, (POLES, GROUPS), jnp.float32) < share
    slow_rate = jnp.exp(jax.random.uniform(slow_key, (POLES, GROUPS), jnp.float32, jnp.log(0.05), jnp.log(2.0))) / TOKENS
    fast_rate = jnp.exp(jax.random.uniform(fast_key, (POLES, GROUPS), jnp.float32, jnp.log(0.02), jnp.log(0.1)))
    return jnp.where(slow_mask, slow_rate, fast_rate)


def levels(rng, extent, pieces, least, high):
    level = 1.0
    for position, shards_of in pieces:
        heights = jax.random.uniform(jax.random.fold_in(jax.random.fold_in(rng, 6), position), (shards_of,), jnp.float32, least / len(pieces), high / len(pieces))
        level = level * jnp.repeat(jnp.exp(heights), extent[position] // shards_of).reshape((-1,) + (1,) * (len(extent) - 1 - position))
    return level


def normal_values(own_key, extent, deviation, most, shards=(), kind=jnp.bfloat16):
    level = levels(own_key, extent, shards, -0.22, 0.18) if shards else 1.0
    values = jax.random.normal(own_key, extent, jnp.float32) * deviation * level
    return jnp.minimum(jnp.maximum(values, -most), most).astype(kind)


def setup_inputs(seed: int = 0) -> dict:
    key_of = jax.random.split(jax.random.key(seed), 11)
    return {
        "resid": draw_resid(jax.random.fold_in(key_of[10], 71), 0),
        "q_mr": normal_values(key_of[1], (TOKENS, D), 1.0, 4.0, ((0, 128), (1, 4))),
        "k_mr": normal_values(key_of[2], (TOKENS, D), 1.0, 4.0, ((0, 128), (1, 4))),
        "v_mr": normal_values(key_of[3], (TOKENS, D), 1.0, 4.0, ((0, 128), (1, 4))),
        "mr_taps": normal_values(key_of[4], (GROUPS, FILT), FILT ** -0.5, 0.5, ((0, 4),)),
        "norm_gain": jnp.clip(1.0 + 0.18 * jax.random.normal(key_of[5], (D,), jnp.float32), 0.099609375, 1.8984375).astype(jnp.bfloat16),
        "q_lr": normal_values(key_of[6], (TOKENS, D), 1.0, 4.0, ((0, 128), (1, 4))),
        "k_lr": normal_values(key_of[7], (TOKENS, D), 1.0, 4.0, ((0, 128), (1, 4))),
        "pole_rate": draw_pole_rate(jax.random.fold_in(key_of[10], 71), 0),
        "residue": normal_values(key_of[9], (POLES, GROUPS), 0.5, 3.0, ((1, 4),), jnp.float32),
    }


HIGHEST_MODE = lax.Precision.HIGHEST

def banded(vector, out_rows):
    length = vector.shape[-1]
    span_cols = out_rows + length - 1
    padding = jnp.zeros(vector.shape[:-1] + (span_cols + 1 - length,), vector.dtype)
    line = jnp.concatenate([vector, padding], axis=-1)
    tiled = jnp.tile(line, (1,) * (vector.ndim - 1) + (out_rows,))
    return tiled[..., :out_rows * span_cols].reshape(vector.shape[:-1] + (out_rows, span_cols))

def modal_tables(pole_rate, residue, tok_rows):
    weights_eff = residue * jnp.sqrt(-jnp.expm1(-2.0 * pole_rate))
    positions = jnp.arange(tok_rows, dtype=jnp.float32)
    powers = jnp.exp(-pole_rate[:, :, None] * positions)
    impulse = lax.optimization_barrier(jnp.sum(weights_eff[:, :, None] * powers, axis=0))
    square = banded(impulse[:, ::-1], tok_rows)[:, :, tok_rows - 1:]
    entry = weights_eff[:, :, None] * powers * jnp.exp(-pole_rate)[:, :, None]
    leaving = powers[:, :, ::-1]
    through = jnp.exp(-pole_rate * tok_rows)
    return (square, entry, leaving, through)

def reference(resid, q_mr, k_mr, v_mr, mr_taps, norm_gain, q_lr, k_lr, pole_rate, residue):
    blocks = TOKENS // TOK_DEV
    window_len = TOK_DEV + FILT - 1
    mr_in = (k_mr.astype(jnp.float32) * v_mr.astype(jnp.float32)).astype(jnp.bfloat16)
    kernel = banded(mr_taps[:, ::-1], TOK_DEV).astype(jnp.float32)
    padded = jnp.concatenate([jnp.zeros((FILT - 1, D), jnp.bfloat16), mr_in], axis=0)

    def mr_block(block):
        start = (block * TOK_DEV).astype(jnp.int32)
        window = lax.dynamic_slice_in_dim(padded, start, window_len, 0)
        window = window.astype(jnp.float32).reshape(window_len, GROUPS, GROUP)
        return jnp.einsum('gtr,rgc->tgc', kernel, window).reshape(TOK_DEV, D)
    mr_conv = lax.map(mr_block, jnp.arange(blocks, dtype=jnp.int32)).reshape(TOKENS, D)
    mixed = (resid.astype(jnp.float32) + q_mr.astype(jnp.float32) * mr_conv).astype(jnp.bfloat16)
    mixed_f = mixed.astype(jnp.float32)
    mean_square = lax.optimization_barrier(jnp.mean(mixed_f * mixed_f, axis=1, keepdims=True))
    normed = mixed_f * lax.rsqrt(mean_square + 1e-06) * norm_gain.astype(jnp.float32)
    lr_in = k_lr.astype(jnp.float32) * normed
    square, entry, leaving, through = modal_tables(pole_rate, residue, TOK_DEV)
    blocks_in = lr_in.reshape(blocks, TOK_DEV, GROUPS, GROUP)

    def lr_step(carried, block_in):
        local = jnp.einsum('gts,sgc->tgc', square, block_in, precision=HIGHEST_MODE)
        incoming = jnp.einsum('pgt,pgc->tgc', entry, carried, precision=HIGHEST_MODE)
        state_end = jnp.einsum('pgs,sgc->pgc', leaving, block_in, precision=HIGHEST_MODE)
        return (through[:, :, None] * carried + state_end, local + incoming)
    start_state = jnp.zeros((POLES, GROUPS, GROUP), jnp.float32)
    _, conv_blocks = lax.scan(lr_step, start_state, blocks_in)
    lr_conv = conv_blocks.reshape(TOKENS, D)
    lr_out = (q_lr.astype(jnp.float32) * lr_conv).astype(jnp.bfloat16)
    return (mixed, lr_out)
```

```python
import functools

import jax
import jax.numpy as jnp
from jax import lax
from jax.experimental import pallas as pl
from jax.experimental.pallas import tpu as pltpu
from jax.sharding import PartitionSpec as P

F32 = jnp.float32
BF16 = jnp.bfloat16
MESH = pl.DeviceIdType.MESH

TOK = 128
LANES = 128
GROUP = 16
PER_TILE = LANES // GROUP
POLES = 16
BLOCK = 16
OWNERS = 8
CHUNKS = 4

OWNER_STEPS = ((1, 2), (0, 2), (1, 1), (1, 3), (0, 1), (0, 3), (1, 0), (0, 0))
BLOCK_STEPS = (4, 3, 5, 2, 6, 1, 7)


def shared_steps(rate, residue):
    y = 2.0 * rate
    series = jnp.ones_like(y)
    for order in range(10, 1, -1):
        series = 1.0 - series * y / order
    gap = jnp.where(y < 0.5, y * series, 1.0 - jnp.exp(-y))
    return residue * jnp.sqrt(gap)


def kernel(
    blocks,
    tp_size,
    resid_h, q_mr_h, k_mr_h, v_mr_h, taps_h, gain_h, q_lr_h, k_lr_h, rate_h, residue_h,
    mixed_h, out_h,
    k_mr, v_mr, resid, q_mr, k_lr, q_lr, taps, gain, rate, residue,
    window, mr_tab, lr_tab, leave_tab, entry_tab, taps_rev, weight_eff, impulse,
    mixed, gated, local, lr_out, squares, states, gathered, total, totals, carry_out, carry_in,
    kv_sem, in_sem, out_sem, halo_send, halo_recv, tp_send, tp_recv,
    own_send, own_recv, tot_send, tot_recv, back_send, back_recv,
):
    me = lax.axis_index("ctx")
    tp = lax.axis_index("tp")
    shards = blocks * BLOCK
    channels = k_mr.shape[1]
    tiles = channels // LANES
    wide = channels // CHUNKS
    block = me // BLOCK
    member = me % BLOCK
    base = block * BLOCK
    core = me % 2
    x_at = (me // 2) % 4
    z_at = (me // 8) % 2
    first = me == 0
    last = me == shards - 1
    is_owner = core == 1

    kv_copies = []
    for c in range(CHUNKS):
        cols = pl.ds(c * wide, wide)
        pair = []
        for i, (src, dst) in enumerate(((k_mr_h, k_mr), (v_mr_h, v_mr))):
            copy = pltpu.make_async_copy(src.at[:, cols], dst.at[:, cols], kv_sem.at[i, c])
            copy.start()
            pair.append(copy)
        kv_copies.append(pair)
    in_copies = {}
    for i, (name, src, dst) in enumerate((
        ("taps", taps_h, taps), ("rate", rate_h, rate), ("residue", residue_h, residue),
        ("resid", resid_h, resid), ("q_mr", q_mr_h, q_mr), ("k_lr", k_lr_h, k_lr),
        ("gain", gain_h, gain), ("q_lr", q_lr_h, q_lr),
    )):
        in_copies[name] = pltpu.make_async_copy(src, dst, in_sem.at[i])
        in_copies[name].start()

    totals[...] = jnp.zeros_like(totals)

    barrier = pltpu.get_barrier_semaphore()

    def greet(ctx, tp_to):
        pl.semaphore_signal(barrier, inc=1, device_id=(ctx, tp_to), device_id_type=MESH)

    @pl.when(jnp.logical_not(last))
    def _():
        greet(me + 1, tp)

    @pl.when(jnp.logical_not(first))
    def _():
        greet(me - 1, tp)

    for d in range(1, tp_size):
        greet(me, (tp + d) % tp_size)
    for dz, dx in OWNER_STEPS:
        chip = base + ((z_at + dz) % 2) * 8 + ((x_at + dx) % 4) * 2
        if (dz, dx) != (0, 0):
            greet(chip + 1, tp)

    @pl.when(is_owner)
    def _():
        for dz, dx in OWNER_STEPS:
            chip = base + ((z_at + dz) % 2) * 8 + ((x_at + dx) % 4) * 2
            greet(chip, tp)
        for d in range(1, blocks):
            greet(((block + d) % blocks) * BLOCK + member, tp)

    @pl.when(jnp.logical_not(is_owner))
    def _():
        greet(me + 1, tp)

    halo = []
    for c in range(CHUNKS):
        for copy in kv_copies[c]:
            copy.wait()
        cols = pl.ds(c * wide, wide)
        window[TOK:, cols] = (k_mr[:, cols].astype(F32) * v_mr[:, cols].astype(F32)).astype(BF16)
        if c == 0:
            ends = jnp.where(first, 0, 1) + jnp.where(last, 0, 1)
            near = jnp.where(is_owner, BLOCK - 1 + blocks - 1, OWNERS)
            pl.semaphore_wait(barrier, ends + near + (tp_size - 1))

        copy = pltpu.make_async_remote_copy(
            src_ref=window.at[pl.ds(TOK, TOK), cols],
            dst_ref=window.at[pl.ds(0, TOK), cols],
            send_sem=halo_send.at[c],
            recv_sem=halo_recv.at[c],
            device_id=(jnp.where(last, me - 1, me + 1), tp),
            device_id_type=MESH,
        )
        halo.append(copy)

        @pl.when(jnp.logical_not(last))
        def _():
            copy.start()

    @pl.when(first)
    def _():
        window[:TOK, :] = jnp.zeros((TOK, channels), BF16)

    row_of = lax.broadcasted_iota(jnp.int32, (TOK, TOK), 0)
    col_of = lax.broadcasted_iota(jnp.int32, (TOK, TOK), 1)
    diagonal = row_of == col_of
    causal = col_of <= row_of
    for name in ("taps", "rate", "residue"):
        in_copies[name].wait()
    flip = ((row_of + col_of) % TOK == 0).astype(BF16)
    taps_rev[...] = jnp.dot(taps[...], flip, preferred_element_type=F32)
    weight_eff[...] = shared_steps(rate[...], residue[...])

    def mr_tables(j, carry):
        for i in range(PER_TILE):
            g = j * PER_TILE + i
            line = jnp.broadcast_to(taps_rev[pl.ds(g, 1), :], (TOK, TOK))
            square = pltpu.roll(line, 0, 1, stride=1, stride_axis=0)
            rows = pl.ds(pl.multiple_of(g * TOK, TOK), TOK)
            mr_tab[rows, :TOK] = jnp.where(causal, 0.0, square).astype(BF16)
            mr_tab[rows, TOK:] = jnp.where(causal, square, 0.0).astype(BF16)
        return carry

    lax.fori_loop(0, tiles, mr_tables, 0, unroll=4)

    row_group = row_of // POLES
    rates = jnp.concatenate([rate[...]] * PER_TILE, axis=0)
    weights = jnp.concatenate([weight_eff[...]] * PER_TILE, axis=0)
    backward = (TOK - 1 - col_of).astype(F32)
    forward = (col_of + 1).astype(F32)

    def of_rows(j, values):
        here = col_of == row_group + j * PER_TILE
        return jnp.sum(jnp.where(here, values, 0.0), axis=1, keepdims=True)

    def leave_table(j, carry):
        leave = jnp.exp(-of_rows(j, rates) * backward)
        rows = pl.ds(pl.multiple_of(j * TOK, TOK), TOK)
        high = leave.astype(BF16)
        leave_tab[rows, :TOK] = high
        leave_tab[rows, TOK:] = (leave - high.astype(F32)).astype(BF16)
        weighted = of_rows(j, weights) * leave
        lines = [
            jnp.sum(weighted[i * POLES : (i + 1) * POLES], axis=0, keepdims=True)
            for i in range(PER_TILE)
        ]
        rows = pl.ds(pl.multiple_of(j * PER_TILE, PER_TILE), PER_TILE)
        impulse[rows, :] = pltpu.roll(jnp.concatenate(lines, axis=0), 1, 1)
        return carry

    lax.fori_loop(0, tiles, leave_table, 0, unroll=4)

    def lr_tables(j, carry):
        for i in range(PER_TILE):
            g = j * PER_TILE + i
            line = jnp.broadcast_to(impulse[pl.ds(g, 1), :], (TOK, TOK))
            square = pltpu.roll(line, 0, 1, stride=1, stride_axis=0)
            rows = pl.ds(pl.multiple_of(g * TOK, TOK), TOK)
            lr_tab[rows, :] = jnp.where(causal, square, 0.0).astype(BF16)
        return carry

    def entry_table(j, carry):
        entry = (of_rows(j, weights) * jnp.exp(-of_rows(j, rates) * forward)).T
        high = entry.astype(BF16)
        rows = pl.ds(pl.multiple_of(j * TOK, TOK), TOK)
        entry_tab[rows, :LANES] = high
        entry_tab[rows, LANES:] = (entry - high.astype(F32)).astype(BF16)
        return carry

    def own_lanes(stacked, rows):
        mask = lax.broadcasted_iota(jnp.int32, (rows, LANES), 1) // GROUP
        out = stacked[:rows]
        for i in range(1, PER_TILE):
            out = jnp.where(mask == i, stacked[i * rows : (i + 1) * rows], out)
        return out

    squares_sum = jnp.zeros((TOK, LANES), F32)
    for name in ("resid", "q_mr"):
        in_copies[name].wait()
    for c in range(CHUNKS):
        @pl.when(jnp.logical_not(first))
        def _():
            halo[c].wait_recv()

        def mr_tile(j, acc):
            cols = pl.ds(pl.multiple_of(j * LANES, LANES), LANES)
            rows = pl.ds(pl.multiple_of(j * PER_TILE * TOK, TOK), PER_TILE * TOK)
            stacked = jnp.dot(mr_tab[rows, :], window[:, cols], preferred_element_type=F32)
            conv = own_lanes(stacked, TOK)
            result = (resid[:, cols].astype(F32) + q_mr[:, cols].astype(F32) * conv).astype(BF16)
            mixed[:, cols] = result
            result = result.astype(F32)
            return acc + result * result

        per_chunk = tiles // CHUNKS
        squares_sum = lax.fori_loop(c * per_chunk, (c + 1) * per_chunk, mr_tile, squares_sum, unroll=True)

    row_sum = jnp.sum(squares_sum, axis=1, keepdims=True)
    line = jnp.sum(jnp.where(diagonal, row_sum, 0.0), axis=0, keepdims=True)
    squares[tp] = jnp.broadcast_to(line, (8, TOK))
    tp_copies = []
    for d in (2, 1, 3):
        copy = pltpu.make_async_remote_copy(
            src_ref=squares.at[tp],
            dst_ref=squares.at[tp],
            send_sem=tp_send.at[d],
            recv_sem=tp_recv.at[d],
            device_id=(me, (tp + d) % tp_size),
            device_id_type=MESH,
        )
        copy.start()
        tp_copies.append(copy)
    mixed_copy = pltpu.make_async_copy(mixed, mixed_h, out_sem.at[0])
    mixed_copy.start()
    for name in ("k_lr", "gain", "q_lr"):
        in_copies[name].wait()

    def gate_tile(j, carry):
        cols = pl.ds(pl.multiple_of(j * LANES, LANES), LANES)
        scaled = mixed[:, cols].astype(F32) * gain[:, cols].astype(F32)
        gated[:, cols] = scaled * k_lr[:, cols].astype(F32)
        return carry

    lax.fori_loop(0, tiles, gate_tile, 0, unroll=4)
    lax.fori_loop(0, tiles, lr_tables, 0, unroll=4)
    lax.fori_loop(0, tiles, entry_table, 0, unroll=4)
    for copy in tp_copies:
        copy.wait_recv()
    line = squares[0, :1, :]
    for d in range(1, tp_size):
        line = line + squares[d, :1, :]
    line = lax.rsqrt(line / (channels * tp_size) + 1e-06)
    scale = jnp.sum(jnp.where(diagonal, line, 0.0), axis=1, keepdims=True)

    lr_in = window

    own_copies = []
    for s, (dz, dx) in enumerate(OWNER_STEPS):
        z_to, x_to = (z_at + dz) % 2, (x_at + dx) % 4
        owner = z_to * 4 + x_to
        for half in range(2):
            j = owner * 2 + half
            cols = pl.ds(pl.multiple_of(j * LANES, LANES), LANES)
            value = (gated[:, cols] * scale).astype(BF16)
            lr_in[:TOK, cols] = value
            rows = pl.ds(pl.multiple_of(j * LANES, LANES), LANES)
            stacked = jnp.dot(
                leave_tab[rows, :], jnp.concatenate([value, value], axis=0), preferred_element_type=F32
            )
            states[s, half * POLES : (half + 1) * POLES, :] = own_lanes(stacked, POLES).astype(BF16)
        copy = pltpu.make_async_remote_copy(
            src_ref=states.at[s],
            dst_ref=gathered.at[member],
            send_sem=own_send.at[s],
            recv_sem=own_recv,
            device_id=(
                jnp.where(is_owner & ((dz, dx) == (0, 0)), me - 1, base + z_to * 8 + x_to * 2 + 1),
                tp,
            ),
            device_id_type=MESH,
        )
        own_copies.append(copy)
        if (dz, dx) == (0, 0):
            @pl.when(is_owner)
            def _():
                gathered[member] = states[s]

            @pl.when(jnp.logical_not(is_owner))
            def _():
                copy.start()
        else:
            copy.start()

    def lr_conv_tile(j, carry):
        cols = pl.ds(pl.multiple_of(j * LANES, LANES), LANES)
        rows = pl.ds(pl.multiple_of(j * PER_TILE * TOK, TOK), PER_TILE * TOK)
        stacked = jnp.dot(lr_tab[rows, :], lr_in[:TOK, cols], preferred_element_type=F32)
        local[:, cols] = own_lanes(stacked, TOK)
        return carry

    lax.fori_loop(0, tiles // 2, lr_conv_tile, 0, unroll=4)

    my_owner = z_at * 4 + x_at

    def total_copy(d, to):
        return pltpu.make_async_remote_copy(
            src_ref=total,
            dst_ref=totals.at[block],
            send_sem=tot_send.at[d],
            recv_sem=tot_recv.at[block],
            device_id=(to * BLOCK + member, tp),
            device_id_type=MESH,
        )

    back_steps = [(dz, dx, c) for dz, dx in OWNER_STEPS for c in (0, 1)]
    back_steps.remove((0, 0, 1))

    @pl.when(is_owner)
    def _():
        lane = lax.broadcasted_iota(jnp.int32, (LANES, 2 * LANES), 1)
        row = lax.broadcasted_iota(jnp.int32, (LANES, 2 * LANES), 0)
        spread = (row == my_owner * 2 * PER_TILE + lane // GROUP).astype(F32)
        wide_rate = jnp.dot(
            rate[...], spread, precision=lax.Precision.HIGHEST, preferred_element_type=F32
        )
        wide_rate = jnp.concatenate([wide_rate[:, :LANES], wide_rate[:, LANES:]], axis=0)
        through = jnp.exp(-wide_rate * TOK)
        through_block = jnp.exp(-wide_rate * (TOK * BLOCK))
        pltpu.make_async_copy(
            gathered.at[pl.ds(0, BLOCK - 1)], gathered.at[pl.ds(0, BLOCK - 1)], own_recv
        ).wait()
        state = jnp.zeros((2 * POLES, LANES), F32)
        for i in range(BLOCK):
            state = state * through + gathered[i].astype(F32)
        total[...] = state.astype(BF16)
        for d in BLOCK_STEPS:
            @pl.when(block + d < blocks)
            def _():
                total_copy(d, block + d).start()

        lax.fori_loop(tiles // 2, tiles, lr_conv_tile, 0, unroll=4)

        carried = jnp.zeros((2 * POLES, LANES), F32)
        for b in range(blocks - 1):
            @pl.when(b < block)
            def _():
                pltpu.make_async_copy(totals.at[b], totals.at[b], tot_recv.at[b]).wait()

        for b in range(blocks - 1):
            carried = jnp.where(b < block, carried * through_block + totals[b].astype(F32), carried)
        for i in range(BLOCK):
            carry_out[i] = carried.astype(BF16)
            if i < BLOCK - 1:
                carried = carried * through + gathered[i].astype(F32)
        for s, (dz, dx, c) in enumerate(back_steps):
            to = ((z_at + dz) % 2) * 8 + ((x_at + dx) % 4) * 2 + c
            pltpu.make_async_remote_copy(
                src_ref=carry_out.at[to],
                dst_ref=carry_in.at[my_owner],
                send_sem=back_send.at[s],
                recv_sem=back_recv,
                device_id=(base + to, tp),
                device_id_type=MESH,
            ).start()
        carry_in[my_owner] = carry_out[member]
        pltpu.make_async_copy(
            carry_in.at[pl.ds(0, OWNERS - 1)], carry_in.at[pl.ds(0, OWNERS - 1)], back_recv
        ).wait()

    @pl.when(jnp.logical_not(is_owner))
    def _():
        lax.fori_loop(tiles // 2, tiles, lr_conv_tile, 0, unroll=4)
        pltpu.make_async_copy(carry_in, carry_in, back_recv).wait()

    lane_group = lax.broadcasted_iota(jnp.int32, (POLES, LANES), 1) // GROUP
    pole_masks = [(lane_group == i).astype(F32).astype(BF16) for i in range(PER_TILE)]

    def out_tile(j, carry):
        cols = pl.ds(pl.multiple_of(j * LANES, LANES), LANES)
        rows = pl.ds(pl.multiple_of(j * TOK, TOK), TOK)
        came = carry_in[j // 2, pl.ds(pl.multiple_of((j % 2) * POLES, POLES), POLES), :]
        spread = [came * mask for mask in pole_masks]
        spread = jnp.concatenate(spread + spread, axis=0)
        incoming = jnp.dot(entry_tab[rows, :], spread, preferred_element_type=F32)
        conv = local[:, cols] + incoming
        lr_out[:, cols] = (q_lr[:, cols].astype(F32) * conv).astype(BF16)
        return carry

    out_copies = []
    for c in range(CHUNKS):
        per_chunk = tiles // CHUNKS
        lax.fori_loop(c * per_chunk, (c + 1) * per_chunk, out_tile, 0, unroll=True)
        cols = pl.ds(c * wide, wide)
        copy = pltpu.make_async_copy(lr_out.at[:, cols], out_h.at[:, cols], out_sem.at[1 + c])
        copy.start()
        out_copies.append(copy)

    for copy in halo:
        @pl.when(jnp.logical_not(last))
        def _():
            copy.wait_send()

    for copy in tp_copies:
        copy.wait_send()
    for (dz, dx), copy in zip(OWNER_STEPS, own_copies):
        if (dz, dx) == (0, 0):
            @pl.when(jnp.logical_not(is_owner))
            def _():
                copy.wait_send()
        else:
            copy.wait_send()

    @pl.when(is_owner)
    def _():
        for d in BLOCK_STEPS:
            @pl.when(block + d < blocks)
            def _():
                total_copy(d, block + d).wait_send()
        for s in range(len(back_steps)):
            pltpu.make_async_copy(carry_out.at[0], carry_out.at[0], back_send.at[s]).wait()

    mixed_copy.wait()
    for copy in out_copies:
        copy.wait()


def per_device(resid, q_mr, k_mr, v_mr, mr_taps, norm_gain, q_lr, k_lr, pole_rate, residue):
    tok, channels = resid.shape
    tp_size = lax.axis_size("tp")
    blocks = lax.axis_size("ctx") // BLOCK
    tiles = channels // LANES
    groups = channels // GROUP
    big = pltpu.VMEM((tok, channels), BF16)
    scratch = [
        big, big, big, big, big, big,
        pltpu.VMEM((groups, TOK), BF16),
        pltpu.VMEM((1, channels), BF16),
        pltpu.VMEM((POLES, groups), F32),
        pltpu.VMEM((POLES, groups), F32),
        pltpu.VMEM((2 * TOK, channels), BF16),
        pltpu.VMEM((groups * TOK, 2 * TOK), BF16),
        pltpu.VMEM((groups * TOK, TOK), BF16),
        pltpu.VMEM((groups * POLES, 2 * TOK), BF16),
        pltpu.VMEM((tiles * TOK, 2 * LANES), BF16),
        pltpu.VMEM((groups, TOK), F32),
        pltpu.VMEM((POLES, groups), F32),
        pltpu.VMEM((groups, TOK), F32),
        big,
        pltpu.VMEM((tok, channels), F32),
        pltpu.VMEM((tok, channels), F32),
        big,
        pltpu.VMEM((tp_size, 8, TOK), F32),
        pltpu.VMEM((OWNERS, 2 * POLES, LANES), BF16),
        pltpu.VMEM((BLOCK, 2 * POLES, LANES), BF16),
        pltpu.VMEM((2 * POLES, LANES), BF16),
        pltpu.VMEM((blocks, 2 * POLES, LANES), BF16),
        pltpu.VMEM((BLOCK, 2 * POLES, LANES), BF16),
        pltpu.VMEM((OWNERS, 2 * POLES, LANES), BF16),
        pltpu.SemaphoreType.DMA((2, CHUNKS)),
        pltpu.SemaphoreType.DMA((8,)),
        pltpu.SemaphoreType.DMA((1 + CHUNKS,)),
        pltpu.SemaphoreType.DMA((CHUNKS,)),
        pltpu.SemaphoreType.DMA((CHUNKS,)),
        pltpu.SemaphoreType.DMA((tp_size,)),
        pltpu.SemaphoreType.DMA((tp_size,)),
        pltpu.SemaphoreType.DMA((OWNERS,)),
        pltpu.SemaphoreType.DMA,
        pltpu.SemaphoreType.DMA((blocks,)),
        pltpu.SemaphoreType.DMA((blocks,)),
        pltpu.SemaphoreType.DMA((2 * OWNERS,)),
        pltpu.SemaphoreType.DMA,
    ]
    anywhere = pl.BlockSpec(memory_space=pl.ANY)
    out = jax.ShapeDtypeStruct((tok, channels), BF16)
    return pl.pallas_call(
        functools.partial(kernel, blocks, tp_size),
        out_shape=(out, out),
        in_specs=[anywhere] * 10,
        out_specs=(anywhere, anywhere),
        scratch_shapes=scratch,
        compiler_params=pltpu.CompilerParams(
            collective_id=0, has_side_effects=True, vmem_limit_bytes=56 * 1024 * 1024
        ),
        name="mixers",
    )(resid, q_mr, k_mr, v_mr, mr_taps, norm_gain.reshape(1, channels), q_lr, k_lr, pole_rate, residue)


def solution(mesh):
    placed = (
        P("ctx", "tp"),
        P("ctx", "tp"),
        P("ctx", "tp"),
        P("ctx", "tp"),
        P("tp", None),
        P("tp"),
        P("ctx", "tp"),
        P("ctx", "tp"),
        P(None, "tp"),
        P(None, "tp"),
    )
    return jax.shard_map(
        per_device,
        mesh=mesh,
        in_specs=placed,
        out_specs=(P("ctx", "tp"), P("ctx", "tp")),
        check_vma=False,
    )
```

```python
import functools

import jax
import jax.numpy as jnp
from jax import lax
from jax.experimental import pallas as pl
from jax.experimental.pallas import tpu as pltpu
from jax.sharding import PartitionSpec as P

F32 = jnp.float32
BF16 = jnp.bfloat16
MESH = pl.DeviceIdType.MESH

TOK = 128
LANES = 128
GROUP = 16
PER_TILE = LANES // GROUP
POLES = 16
BLOCK = 16
OWNERS = 8
CHUNKS = (4, 4, 4, 2, 2)

HAND_PIECES = 4

OWNER_STEPS = ((1, 2), (0, 2), (1, 1), (1, 3), (0, 1), (0, 3), (1, 0), (0, 0))
BLOCK_STEPS = (4, 3, 5, 2, 6, 1, 7)


def shared_steps(rate, residue):
    y = 2.0 * rate
    series = jnp.ones_like(y)
    for order in range(10, 1, -1):
        series = 1.0 - series * y / order
    gap = jnp.where(y < 0.5, y * series, 1.0 - jnp.exp(-y))
    return residue * jnp.sqrt(gap)


def kernel(
    blocks,
    tp_size,
    resid_h, q_mr_h, k_mr_h, v_mr_h, taps_h, gain_h, q_lr_h, k_lr_h, rate_h, residue_h,
    mixed, lr_out,
    k_mr, v_mr, resid, q_mr, k_lr, q_lr, taps, gain, gain_in, rate, residue,
    window, mr_tab, lr_tab, leave_tab, entry_tab, taps_rev, weight_eff, impulse,
    gated, local, squares, states, gathered, total, totals, carry_out, carry_in,
    kv_sem, in_sem, halo_send, halo_recv, tp_send, tp_recv,
    own_send, own_recv, tot_send, tot_recv, back_send, back_recv, relay,
):
    me = lax.axis_index("ctx")
    tp = lax.axis_index("tp")
    shards = blocks * BLOCK
    channels = k_mr.shape[1]
    tiles = channels // LANES
    starts = [sum(CHUNKS[:c]) for c in range(len(CHUNKS))]
    block = me // BLOCK
    member = me % BLOCK
    base = block * BLOCK
    core = me % 2
    x_at = (me // 2) % 4
    z_at = (me // 8) % 2
    first = me == 0
    last = me == shards - 1
    is_owner = core == 1

    kv_copies = []
    for c in range(len(CHUNKS)):
        cols = pl.ds(starts[c] * LANES, CHUNKS[c] * LANES)
        pair = []
        for i, (src, dst) in enumerate(((k_mr_h, k_mr), (v_mr_h, v_mr))):
            copy = pltpu.make_async_copy(src.at[:, cols], dst.at[:, cols], kv_sem.at[i, c])
            copy.start()
            pair.append(copy)
        kv_copies.append(pair)
    in_copies = {}
    for i, (name, src, dst) in enumerate((
        ("taps", taps_h, taps), ("rate", rate_h, rate), ("residue", residue_h, residue),
        ("resid", resid_h, resid), ("q_mr", q_mr_h, q_mr), ("k_lr", k_lr_h, k_lr),
        ("gain", gain_h, gain_in), ("q_lr", q_lr_h, q_lr),
    )):
        in_copies[name] = pltpu.make_async_copy(src, dst, in_sem.at[i])
        in_copies[name].start()

    totals[...] = jnp.zeros_like(totals)

    barrier = pltpu.get_barrier_semaphore()

    def greet(ctx, tp_to):
        pl.semaphore_signal(barrier, inc=1, device_id=(ctx, tp_to), device_id_type=MESH)

    @pl.when(jnp.logical_not(last))
    def _():
        greet(me + 1, tp)

    @pl.when(jnp.logical_not(first))
    def _():
        greet(me - 1, tp)

    for d in range(1, tp_size):
        greet(me, (tp + d) % tp_size)
    for dz, dx in OWNER_STEPS:
        chip = base + ((z_at + dz) % 2) * 8 + ((x_at + dx) % 4) * 2
        if (dz, dx) != (0, 0):
            greet(chip + 1, tp)

    @pl.when(is_owner)
    def _():
        for dz, dx in OWNER_STEPS:
            chip = base + ((z_at + dz) % 2) * 8 + ((x_at + dx) % 4) * 2
            greet(chip, tp)
        greet(((block + 1) % blocks) * BLOCK + member, tp)
        greet(((block + blocks - 1) % blocks) * BLOCK + member, tp)

    @pl.when(jnp.logical_not(is_owner))
    def _():
        greet(me + 1, tp)

    halo = []
    for c in range(len(CHUNKS)):
        for copy in kv_copies[c]:
            copy.wait()
        cols = pl.ds(starts[c] * LANES, CHUNKS[c] * LANES)
        window[TOK:, cols] = (k_mr[:, cols].astype(F32) * v_mr[:, cols].astype(F32)).astype(BF16)
        if c == 0:
            ends = jnp.where(first, 0, 1) + jnp.where(last, 0, 1)
            near = jnp.where(is_owner, BLOCK - 1 + 2, OWNERS)
            pl.semaphore_wait(barrier, ends + near + (tp_size - 1))

        copy = pltpu.make_async_remote_copy(
            src_ref=window.at[pl.ds(TOK, TOK), cols],
            dst_ref=window.at[pl.ds(0, TOK), cols],
            send_sem=halo_send.at[c],
            recv_sem=halo_recv.at[c],
            device_id=(jnp.where(last, me - 1, me + 1), tp),
            device_id_type=MESH,
        )
        halo.append(copy)

        @pl.when(jnp.logical_not(last))
        def _():
            copy.start()

    @pl.when(first)
    def _():
        window[:TOK, :] = jnp.zeros((TOK, channels), BF16)

    def pass_on(step):
        @pl.when(is_owner)
        def _():
            for d in (step, blocks - step):
                pl.semaphore_signal(
                    relay.at[step - 1], inc=1,
                    device_id=(((block + d) % blocks) * BLOCK + member, tp), device_id_type=MESH,
                )

    def hear(step):
        @pl.when(is_owner)
        def _():
            pl.semaphore_wait(relay.at[step - 1], 2)

    pass_on(1)

    row_of = lax.broadcasted_iota(jnp.int32, (TOK, TOK), 0)
    col_of = lax.broadcasted_iota(jnp.int32, (TOK, TOK), 1)
    diagonal = row_of == col_of
    causal = col_of <= row_of
    for name in ("taps", "rate", "residue"):
        in_copies[name].wait()
    flip = ((row_of + col_of) % TOK == 0).astype(BF16)
    taps_rev[...] = jnp.dot(taps[...], flip, preferred_element_type=F32)
    weight_eff[...] = shared_steps(rate[...], residue[...])

    def mr_tables(j, carry):
        for i in range(PER_TILE):
            g = j * PER_TILE + i
            line = jnp.broadcast_to(taps_rev[pl.ds(g, 1), :], (TOK, TOK))
            square = pltpu.roll(line, 0, 1, stride=1, stride_axis=0)
            rows = pl.ds(pl.multiple_of(g * TOK, TOK), TOK)
            mr_tab[rows, :TOK] = jnp.where(causal, 0.0, square).astype(BF16)
            mr_tab[rows, TOK:] = jnp.where(causal, square, 0.0).astype(BF16)
        return carry

    lax.fori_loop(0, tiles, mr_tables, 0, unroll=4)

    row_group = row_of // POLES
    rates = jnp.concatenate([rate[...]] * PER_TILE, axis=0)
    weights = jnp.concatenate([weight_eff[...]] * PER_TILE, axis=0)
    backward = (TOK - 1 - col_of).astype(F32)
    forward = (col_of + 1).astype(F32)

    def of_rows(j, values):
        here = col_of == row_group + j * PER_TILE
        return jnp.sum(jnp.where(here, values, 0.0), axis=1, keepdims=True)

    def leave_table(j, carry):
        leave = jnp.exp(-of_rows(j, rates) * backward)
        rows = pl.ds(pl.multiple_of(j * TOK, TOK), TOK)
        high = leave.astype(BF16)
        leave_tab[rows, :TOK] = high
        leave_tab[rows, TOK : 2 * TOK] = (leave - high.astype(F32)).astype(BF16)
        leave_tab[rows, 2 * TOK :] = high
        weighted = of_rows(j, weights) * leave
        lines = [
            jnp.sum(weighted[i * POLES : (i + 1) * POLES], axis=0, keepdims=True)
            for i in range(PER_TILE)
        ]
        rows = pl.ds(pl.multiple_of(j * PER_TILE, PER_TILE), PER_TILE)
        impulse[rows, :] = pltpu.roll(jnp.concatenate(lines, axis=0), 1, 1)
        return carry

    lax.fori_loop(0, tiles, leave_table, 0, unroll=4)

    def lr_tables(j, carry):
        for i in range(PER_TILE):
            g = j * PER_TILE + i
            line = jnp.broadcast_to(impulse[pl.ds(g, 1), :], (TOK, TOK))
            square = pltpu.roll(line, 0, 1, stride=1, stride_axis=0)
            rows = pl.ds(pl.multiple_of(g * TOK, TOK), TOK)
            square = jnp.where(causal, square, 0.0)
            high = square.astype(BF16)
            lr_tab[rows, :TOK] = high
            lr_tab[rows, TOK : 2 * TOK] = (square - high.astype(F32)).astype(BF16)
            lr_tab[rows, 2 * TOK :] = high
        return carry

    def entry_table(j, carry):
        entry = (of_rows(j, weights) * jnp.exp(-of_rows(j, rates) * forward)).T
        high = entry.astype(BF16)
        rows = pl.ds(pl.multiple_of(j * TOK, TOK), TOK)
        entry_tab[rows, :LANES] = high
        entry_tab[rows, LANES:] = (entry - high.astype(F32)).astype(BF16)
        return carry

    def own_lanes(stacked, rows):
        mask = lax.broadcasted_iota(jnp.int32, (rows, LANES), 1) // GROUP
        out = stacked[:rows]
        for i in range(1, PER_TILE):
            out = jnp.where(mask == i, stacked[i * rows : (i + 1) * rows], out)
        return out

    hear(1)
    pass_on(2)

    squares_sum = jnp.zeros((TOK, LANES), F32)
    for name in ("resid", "q_mr"):
        in_copies[name].wait()
    for c in range(len(CHUNKS)):
        @pl.when(jnp.logical_not(first))
        def _():
            halo[c].wait_recv()

        def mr_tile(j, acc):
            cols = pl.ds(pl.multiple_of(j * LANES, LANES), LANES)
            rows = pl.ds(pl.multiple_of(j * PER_TILE * TOK, TOK), PER_TILE * TOK)
            stacked = jnp.dot(mr_tab[rows, :], window[:, cols], preferred_element_type=F32)
            conv = own_lanes(stacked, TOK)
            result = (resid[:, cols].astype(F32) + q_mr[:, cols].astype(F32) * conv).astype(BF16)
            mixed[:, cols] = result
            result = result.astype(F32)
            return acc + result * result

        squares_sum = lax.fori_loop(starts[c], starts[c] + CHUNKS[c], mr_tile, squares_sum, unroll=True)

    row_sum = jnp.sum(squares_sum, axis=1, keepdims=True)
    line = jnp.sum(jnp.where(diagonal, row_sum, 0.0), axis=0, keepdims=True)
    squares[tp] = jnp.broadcast_to(line, (8, TOK))
    tp_copies = []
    for d in (2, 1, 3):
        copy = pltpu.make_async_remote_copy(
            src_ref=squares.at[tp],
            dst_ref=squares.at[tp],
            send_sem=tp_send.at[d],
            recv_sem=tp_recv.at[d],
            device_id=(me, (tp + d) % tp_size),
            device_id_type=MESH,
        )
        copy.start()
        tp_copies.append(copy)
    for name in ("k_lr", "gain", "q_lr"):
        in_copies[name].wait()

    gain[...] = gain_in[...].astype(F32)

    def gate_tile(j, carry):
        cols = pl.ds(pl.multiple_of(j * LANES, LANES), LANES)
        scaled = mixed[:, cols].astype(F32) * gain[pl.ds(j, 1), :]
        gated[:, cols] = scaled * k_lr[:, cols].astype(F32)
        return carry

    lax.fori_loop(0, tiles, gate_tile, 0, unroll=4)
    lax.fori_loop(0, tiles, lr_tables, 0, unroll=4)
    for copy in tp_copies:
        copy.wait_recv()
    line = squares[0, :1, :]
    for d in range(1, tp_size):
        line = line + squares[d, :1, :]
    line = lax.rsqrt(line / (channels * tp_size) + 1e-06)
    scale = jnp.sum(jnp.where(diagonal, line, 0.0), axis=1, keepdims=True)

    lr_in = window

    for copy in halo:
        @pl.when(jnp.logical_not(last))
        def _():
            copy.wait_send()

    own_copies = []
    for s, (dz, dx) in enumerate(OWNER_STEPS):
        z_to, x_to = (z_at + dz) % 2, (x_at + dx) % 4
        owner = z_to * 4 + x_to
        for half in range(2):
            j = owner * 2 + half
            cols = pl.ds(pl.multiple_of(j * LANES, LANES), LANES)
            value = gated[:, cols] * scale
            high = value.astype(BF16)
            low = (value - high.astype(F32)).astype(BF16)
            lr_in[:TOK, cols] = high
            lr_in[TOK:, cols] = low
            rows = pl.ds(pl.multiple_of(j * LANES, LANES), LANES)
            stacked = jnp.dot(
                leave_tab[rows, :],
                jnp.concatenate([high, high, low], axis=0),
                preferred_element_type=F32,
            )
            states[s, half * POLES : (half + 1) * POLES, :] = own_lanes(stacked, POLES).astype(BF16)
        copy = pltpu.make_async_remote_copy(
            src_ref=states.at[s],
            dst_ref=gathered.at[member],
            send_sem=own_send.at[s],
            recv_sem=own_recv,
            device_id=(
                jnp.where(is_owner & ((dz, dx) == (0, 0)), me - 1, base + z_to * 8 + x_to * 2 + 1),
                tp,
            ),
            device_id_type=MESH,
        )
        own_copies.append(copy)
        if (dz, dx) == (0, 0):
            @pl.when(is_owner)
            def _():
                gathered[member] = states[s]

            @pl.when(jnp.logical_not(is_owner))
            def _():
                copy.start()
        else:
            copy.start()

    def lr_conv_tile(j, carry):
        cols = pl.ds(pl.multiple_of(j * LANES, LANES), LANES)
        rows = pl.ds(pl.multiple_of(j * PER_TILE * TOK, TOK), PER_TILE * TOK)
        high, low = lr_in[:TOK, cols], lr_in[TOK:, cols]
        stacked = jnp.dot(
            lr_tab[rows, :], jnp.concatenate([high, high, low], axis=0), preferred_element_type=F32
        )
        local[:, cols] = own_lanes(stacked, TOK)
        return carry

    lax.fori_loop(0, tiles // 2, lr_conv_tile, 0, unroll=4)

    hear(2)

    my_owner = z_at * 4 + x_at

    def total_copy(d, to):
        return pltpu.make_async_remote_copy(
            src_ref=total,
            dst_ref=totals.at[block],
            send_sem=tot_send.at[d],
            recv_sem=tot_recv.at[block],
            device_id=(to * BLOCK + member, tp),
            device_id_type=MESH,
        )

    back_steps = [(dz, dx, c) for dz, dx in OWNER_STEPS for c in (0, 1)]
    back_steps.remove((0, 0, 1))

    @pl.when(is_owner)
    def _():
        lane = lax.broadcasted_iota(jnp.int32, (LANES, 2 * LANES), 1)
        row = lax.broadcasted_iota(jnp.int32, (LANES, 2 * LANES), 0)
        spread = (row == my_owner * 2 * PER_TILE + lane // GROUP).astype(F32)
        wide_rate = jnp.dot(
            rate[...], spread, precision=lax.Precision.HIGHEST, preferred_element_type=F32
        )
        wide_rate = jnp.concatenate([wide_rate[:, :LANES], wide_rate[:, LANES:]], axis=0)
        through = jnp.exp(-wide_rate * TOK)
        through_block = jnp.exp(-wide_rate * (TOK * BLOCK))
        pltpu.make_async_copy(
            gathered.at[pl.ds(0, BLOCK - 1)], gathered.at[pl.ds(0, BLOCK - 1)], own_recv
        ).wait()
        state = jnp.zeros((2 * POLES, LANES), F32)
        for i in range(BLOCK):
            state = state * through + gathered[i].astype(F32)
        total[...] = state.astype(BF16)
        for d in BLOCK_STEPS:
            @pl.when(block + d < blocks)
            def _():
                total_copy(d, block + d).start()

        lax.fori_loop(tiles // 2, tiles, lr_conv_tile, 0, unroll=4)
        lax.fori_loop(0, tiles, entry_table, 0, unroll=4)

        carried = jnp.zeros((2 * POLES, LANES), F32)
        for b in range(blocks - 1):
            @pl.when(b < block)
            def _():
                pltpu.make_async_copy(totals.at[b], totals.at[b], tot_recv.at[b]).wait()

        for b in range(blocks - 1):
            carried = jnp.where(b < block, carried * through_block + totals[b].astype(F32), carried)
        for i in range(BLOCK):
            carry_out[i] = carried.astype(BF16)
            if i < BLOCK - 1:
                carried = carried * through + gathered[i].astype(F32)
        for s, (dz, dx, c) in enumerate(back_steps):
            to = ((z_at + dz) % 2) * 8 + ((x_at + dx) % 4) * 2 + c
            pltpu.make_async_remote_copy(
                src_ref=carry_out.at[to],
                dst_ref=carry_in.at[my_owner],
                send_sem=back_send.at[s],
                recv_sem=back_recv,
                device_id=(base + to, tp),
                device_id_type=MESH,
            ).start()
        carry_in[my_owner] = carry_out[member]
        pltpu.make_async_copy(
            carry_in.at[pl.ds(0, OWNERS - 1)], carry_in.at[pl.ds(0, OWNERS - 1)], back_recv
        ).wait()

    @pl.when(jnp.logical_not(is_owner))
    def _():
        lax.fori_loop(tiles // 2, tiles, lr_conv_tile, 0, unroll=4)
        lax.fori_loop(0, tiles, entry_table, 0, unroll=4)
        pltpu.make_async_copy(carry_in, carry_in, back_recv).wait()

    lane_group = lax.broadcasted_iota(jnp.int32, (POLES, LANES), 1) // GROUP
    pole_masks = [(lane_group == i).astype(F32).astype(BF16) for i in range(PER_TILE)]

    def out_tile(j, carry):
        cols = pl.ds(pl.multiple_of(j * LANES, LANES), LANES)
        rows = pl.ds(pl.multiple_of(j * TOK, TOK), TOK)
        came = carry_in[j // 2, pl.ds(pl.multiple_of((j % 2) * POLES, POLES), POLES), :]
        spread = [came * mask for mask in pole_masks]
        spread = jnp.concatenate(spread + spread, axis=0)
        incoming = jnp.dot(entry_tab[rows, :], spread, preferred_element_type=F32)
        conv = local[:, cols] + incoming
        lr_out[:, cols] = (q_lr[:, cols].astype(F32) * conv).astype(BF16)
        return carry

    lax.fori_loop(0, tiles, out_tile, 0, unroll=True)

    for copy in tp_copies:
        copy.wait_send()
    for (dz, dx), copy in zip(OWNER_STEPS, own_copies):
        if (dz, dx) == (0, 0):
            @pl.when(jnp.logical_not(is_owner))
            def _():
                copy.wait_send()
        else:
            copy.wait_send()

    @pl.when(is_owner)
    def _():
        for d in BLOCK_STEPS:
            @pl.when(block + d < blocks)
            def _():
                total_copy(d, block + d).wait_send()
        for s in range(len(back_steps)):
            pltpu.make_async_copy(carry_out.at[0], carry_out.at[0], back_send.at[s]).wait()


def hand_over(mixed, lr_out, mixed_to, lr_out_to, sems):
    rows = TOK // HAND_PIECES
    copies = []
    for i, (src, dst) in enumerate(((mixed, mixed_to), (lr_out, lr_out_to))):
        for c in range(HAND_PIECES):
            part = pl.ds(c * rows, rows)
            copies.append(pltpu.make_async_copy(src.at[part], dst.at[part], sems.at[i, c]))
    for copy in copies:
        copy.start()
    for copy in copies:
        copy.wait()


def per_device(resid, q_mr, k_mr, v_mr, mr_taps, norm_gain, q_lr, k_lr, pole_rate, residue):
    tok, channels = resid.shape
    tp_size = lax.axis_size("tp")
    blocks = lax.axis_size("ctx") // BLOCK
    tiles = channels // LANES
    groups = channels // GROUP
    big = pltpu.VMEM((tok, channels), BF16)
    scratch = [
        big, big, big, big, big, big,
        pltpu.VMEM((groups, TOK), BF16),
        pltpu.VMEM((tiles, LANES), F32),
        pltpu.VMEM((tiles, LANES), BF16),
        pltpu.VMEM((POLES, groups), F32),
        pltpu.VMEM((POLES, groups), F32),
        pltpu.VMEM((2 * TOK, channels), BF16),
        pltpu.VMEM((groups * TOK, 2 * TOK), BF16),
        pltpu.VMEM((groups * TOK, 3 * TOK), BF16),
        pltpu.VMEM((groups * POLES, 3 * TOK), BF16),
        pltpu.VMEM((tiles * TOK, 2 * LANES), BF16),
        pltpu.VMEM((groups, TOK), F32),
        pltpu.VMEM((POLES, groups), F32),
        pltpu.VMEM((groups, TOK), F32),
        pltpu.VMEM((tok, channels), F32),
        pltpu.VMEM((tok, channels), F32),
        pltpu.VMEM((tp_size, 8, TOK), F32),
        pltpu.VMEM((OWNERS, 2 * POLES, LANES), BF16),
        pltpu.VMEM((BLOCK, 2 * POLES, LANES), BF16),
        pltpu.VMEM((2 * POLES, LANES), BF16),
        pltpu.VMEM((blocks, 2 * POLES, LANES), BF16),
        pltpu.VMEM((BLOCK, 2 * POLES, LANES), BF16),
        pltpu.VMEM((OWNERS, 2 * POLES, LANES), BF16),
        pltpu.SemaphoreType.DMA((2, len(CHUNKS))),
        pltpu.SemaphoreType.DMA((8,)),
        pltpu.SemaphoreType.DMA((len(CHUNKS),)),
        pltpu.SemaphoreType.DMA((len(CHUNKS),)),
        pltpu.SemaphoreType.DMA((tp_size,)),
        pltpu.SemaphoreType.DMA((tp_size,)),
        pltpu.SemaphoreType.DMA((OWNERS,)),
        pltpu.SemaphoreType.DMA,
        pltpu.SemaphoreType.DMA((blocks,)),
        pltpu.SemaphoreType.DMA((blocks,)),
        pltpu.SemaphoreType.DMA((2 * OWNERS,)),
        pltpu.SemaphoreType.DMA,
        pltpu.SemaphoreType.REGULAR((2,)),
    ]
    in_place = pl.BlockSpec(memory_space=pl.ANY)
    out = jax.ShapeDtypeStruct((tok, channels), BF16)
    results = pl.pallas_call(
        functools.partial(kernel, blocks, tp_size),
        out_shape=(out, out),
        in_specs=[in_place] * 10,
        out_specs=(pl.BlockSpec(memory_space=pltpu.VMEM),) * 2,
        scratch_shapes=scratch,
        compiler_params=pltpu.CompilerParams(
            collective_id=0, has_side_effects=True, vmem_limit_bytes=56 * 1024 * 1024
        ),
        name="mixers",
    )(resid, q_mr, k_mr, v_mr, mr_taps, norm_gain.reshape(tiles, LANES), q_lr, k_lr, pole_rate, residue)
    return pl.pallas_call(
        hand_over,
        out_shape=(out, out),
        in_specs=[in_place] * 2,
        out_specs=(in_place, in_place),
        scratch_shapes=[pltpu.SemaphoreType.DMA((2, HAND_PIECES))],
        name="hand_over",
    )(*results)


def solution(mesh):
    placed = (
        P("ctx", "tp"),
        P("ctx", "tp"),
        P("ctx", "tp"),
        P("ctx", "tp"),
        P("tp", None),
        P("tp"),
        P("ctx", "tp"),
        P("ctx", "tp"),
        P(None, "tp"),
        P(None, "tp"),
    )
    return jax.shard_map(
        per_device,
        mesh=mesh,
        in_specs=placed,
        out_specs=(P("ctx", "tp"), P("ctx", "tp")),
        check_vma=False,
    )
```

```python
import functools

import jax
import jax.numpy as jnp
from jax import lax
from jax.experimental import pallas as pl
from jax.experimental.pallas import tpu as pltpu
from jax.sharding import PartitionSpec as P

F32 = jnp.float32
BF16 = jnp.bfloat16
MESH = pl.DeviceIdType.MESH

TOK = 128
LANES = 128
GROUP = 16
PER_TILE = LANES // GROUP
POLES = 16
BLOCK = 16
OWNERS = 8
CHUNKS = (4, 4, 4, 2, 2)

HAND_PIECES = 4

OWNER_STEPS = ((1, 2), (0, 2), (1, 1), (1, 3), (0, 1), (0, 3), (1, 0), (0, 0))
BLOCK_STEPS = (4, 3, 5, 2, 6, 1, 7)


def shared_steps(rate, residue):
    y = 2.0 * rate
    series = jnp.ones_like(y)
    for order in range(10, 1, -1):
        series = 1.0 - series * y / order
    gap = jnp.where(y < 0.5, y * series, 1.0 - jnp.exp(-y))
    return residue * jnp.sqrt(gap)


def kernel(
    blocks,
    tp_size,
    resid_h, q_mr_h, k_mr_h, v_mr_h, taps_h, gain_h, q_lr_h, k_lr_h, rate_h, residue_h,
    mixed_h, out_h,
    k_mr, v_mr, resid, q_mr, k_lr, q_lr, taps, gain, gain_in, rate, residue,
    window, mr_tab, lr_tab, leave_tab, entry_tab, taps_rev, weight_eff, impulse,
    mixed, gated, local, lr_out, squares, states, gathered, total, totals, carry_out, carry_in,
    kv_sem, in_sem, out_sem, halo_send, halo_recv, tp_send, tp_recv,
    own_send, own_recv, tot_send, tot_recv, back_send, back_recv, relay,
):
    me = lax.axis_index("ctx")
    tp = lax.axis_index("tp")
    shards = blocks * BLOCK
    channels = k_mr.shape[1]
    tiles = channels // LANES
    starts = [sum(CHUNKS[:c]) for c in range(len(CHUNKS))]
    block = me // BLOCK
    member = me % BLOCK
    base = block * BLOCK
    core = me % 2
    x_at = (me // 2) % 4
    z_at = (me // 8) % 2
    first = me == 0
    last = me == shards - 1
    is_owner = core == 1

    kv_copies = []
    for c in range(len(CHUNKS)):
        cols = pl.ds(starts[c] * LANES, CHUNKS[c] * LANES)
        pair = []
        for i, (src, dst) in enumerate(((k_mr_h, k_mr), (v_mr_h, v_mr))):
            copy = pltpu.make_async_copy(src.at[:, cols], dst.at[:, cols], kv_sem.at[i, c])
            copy.start()
            pair.append(copy)
        kv_copies.append(pair)
    in_copies = {}
    for i, (name, src, dst) in enumerate((
        ("taps", taps_h, taps), ("rate", rate_h, rate), ("residue", residue_h, residue),
        ("resid", resid_h, resid), ("q_mr", q_mr_h, q_mr), ("k_lr", k_lr_h, k_lr),
        ("gain", gain_h, gain_in), ("q_lr", q_lr_h, q_lr),
    )):
        in_copies[name] = pltpu.make_async_copy(src, dst, in_sem.at[i])
        in_copies[name].start()

    totals[...] = jnp.zeros_like(totals)

    barrier = pltpu.get_barrier_semaphore()

    def greet(ctx, tp_to):
        pl.semaphore_signal(barrier, inc=1, device_id=(ctx, tp_to), device_id_type=MESH)

    @pl.when(jnp.logical_not(last))
    def _():
        greet(me + 1, tp)

    @pl.when(jnp.logical_not(first))
    def _():
        greet(me - 1, tp)

    for d in range(1, tp_size):
        greet(me, (tp + d) % tp_size)
    for dz, dx in OWNER_STEPS:
        chip = base + ((z_at + dz) % 2) * 8 + ((x_at + dx) % 4) * 2
        if (dz, dx) != (0, 0):
            greet(chip + 1, tp)

    @pl.when(is_owner)
    def _():
        for dz, dx in OWNER_STEPS:
            chip = base + ((z_at + dz) % 2) * 8 + ((x_at + dx) % 4) * 2
            greet(chip, tp)
        greet(((block + 1) % blocks) * BLOCK + member, tp)
        greet(((block + blocks - 1) % blocks) * BLOCK + member, tp)

    @pl.when(jnp.logical_not(is_owner))
    def _():
        greet(me + 1, tp)

    halo = []
    for c in range(len(CHUNKS)):
        for copy in kv_copies[c]:
            copy.wait()
        cols = pl.ds(starts[c] * LANES, CHUNKS[c] * LANES)
        window[TOK:, cols] = (k_mr[:, cols].astype(F32) * v_mr[:, cols].astype(F32)).astype(BF16)
        if c == 0:
            ends = jnp.where(first, 0, 1) + jnp.where(last, 0, 1)
            near = jnp.where(is_owner, BLOCK - 1 + 2, OWNERS)
            pl.semaphore_wait(barrier, ends + near + (tp_size - 1))

        copy = pltpu.make_async_remote_copy(
            src_ref=window.at[pl.ds(TOK, TOK), cols],
            dst_ref=window.at[pl.ds(0, TOK), cols],
            send_sem=halo_send.at[c],
            recv_sem=halo_recv.at[c],
            device_id=(jnp.where(last, me - 1, me + 1), tp),
            device_id_type=MESH,
        )
        halo.append(copy)

        @pl.when(jnp.logical_not(last))
        def _():
            copy.start()

    @pl.when(first)
    def _():
        window[:TOK, :] = jnp.zeros((TOK, channels), BF16)

    def pass_on(step):
        @pl.when(is_owner)
        def _():
            for d in (step, blocks - step):
                pl.semaphore_signal(
                    relay.at[step - 1], inc=1,
                    device_id=(((block + d) % blocks) * BLOCK + member, tp), device_id_type=MESH,
                )

    def hear(step):
        @pl.when(is_owner)
        def _():
            pl.semaphore_wait(relay.at[step - 1], 2)

    pass_on(1)

    row_of = lax.broadcasted_iota(jnp.int32, (TOK, TOK), 0)
    col_of = lax.broadcasted_iota(jnp.int32, (TOK, TOK), 1)
    diagonal = row_of == col_of
    causal = col_of <= row_of
    for name in ("taps", "rate", "residue"):
        in_copies[name].wait()
    flip = ((row_of + col_of) % TOK == 0).astype(BF16)
    taps_rev[...] = jnp.dot(taps[...], flip, preferred_element_type=F32)
    weight_eff[...] = shared_steps(rate[...], residue[...])

    def mr_tables(j, carry):
        for i in range(PER_TILE):
            g = j * PER_TILE + i
            line = jnp.broadcast_to(taps_rev[pl.ds(g, 1), :], (TOK, TOK))
            square = pltpu.roll(line, 0, 1, stride=1, stride_axis=0)
            rows = pl.ds(pl.multiple_of(g * TOK, TOK), TOK)
            mr_tab[rows, :TOK] = jnp.where(causal, 0.0, square).astype(BF16)
            mr_tab[rows, TOK:] = jnp.where(causal, square, 0.0).astype(BF16)
        return carry

    lax.fori_loop(0, tiles, mr_tables, 0, unroll=4)

    row_group = row_of // POLES
    rates = jnp.concatenate([rate[...]] * PER_TILE, axis=0)
    weights = jnp.concatenate([weight_eff[...]] * PER_TILE, axis=0)
    backward = (TOK - 1 - col_of).astype(F32)
    forward = (col_of + 1).astype(F32)

    def of_rows(j, values):
        here = col_of == row_group + j * PER_TILE
        return jnp.sum(jnp.where(here, values, 0.0), axis=1, keepdims=True)

    def leave_table(j, carry):
        leave = jnp.exp(-of_rows(j, rates) * backward)
        rows = pl.ds(pl.multiple_of(j * TOK, TOK), TOK)
        high = leave.astype(BF16)
        leave_tab[rows, :TOK] = high
        leave_tab[rows, TOK : 2 * TOK] = (leave - high.astype(F32)).astype(BF16)
        leave_tab[rows, 2 * TOK :] = high
        weighted = of_rows(j, weights) * leave
        lines = [
            jnp.sum(weighted[i * POLES : (i + 1) * POLES], axis=0, keepdims=True)
            for i in range(PER_TILE)
        ]
        rows = pl.ds(pl.multiple_of(j * PER_TILE, PER_TILE), PER_TILE)
        impulse[rows, :] = pltpu.roll(jnp.concatenate(lines, axis=0), 1, 1)
        return carry

    def lr_tables(j, carry):
        for i in range(PER_TILE):
            g = j * PER_TILE + i
            line = jnp.broadcast_to(impulse[pl.ds(g, 1), :], (TOK, TOK))
            square = pltpu.roll(line, 0, 1, stride=1, stride_axis=0)
            rows = pl.ds(pl.multiple_of(g * TOK, TOK), TOK)
            square = jnp.where(causal, square, 0.0)
            high = square.astype(BF16)
            lr_tab[rows, :TOK] = high
            lr_tab[rows, TOK : 2 * TOK] = (square - high.astype(F32)).astype(BF16)
            lr_tab[rows, 2 * TOK :] = high
        return carry

    def entry_table(j, carry):
        entry = (of_rows(j, weights) * jnp.exp(-of_rows(j, rates) * forward)).T
        high = entry.astype(BF16)
        rows = pl.ds(pl.multiple_of(j * TOK, TOK), TOK)
        entry_tab[rows, :LANES] = high
        entry_tab[rows, LANES:] = (entry - high.astype(F32)).astype(BF16)
        return carry

    def own_lanes(stacked, rows):
        mask = lax.broadcasted_iota(jnp.int32, (rows, LANES), 1) // GROUP
        out = stacked[:rows]
        for i in range(1, PER_TILE):
            out = jnp.where(mask == i, stacked[i * rows : (i + 1) * rows], out)
        return out

    hear(1)
    pass_on(2)

    squares_sum = jnp.zeros((TOK, LANES), F32)
    for name in ("resid", "q_mr"):
        in_copies[name].wait()
    for c in range(len(CHUNKS)):
        @pl.when(jnp.logical_not(first))
        def _():
            halo[c].wait_recv()

        def mr_tile(j, acc):
            cols = pl.ds(pl.multiple_of(j * LANES, LANES), LANES)
            rows = pl.ds(pl.multiple_of(j * PER_TILE * TOK, TOK), PER_TILE * TOK)
            stacked = jnp.dot(mr_tab[rows, :], window[:, cols], preferred_element_type=F32)
            conv = own_lanes(stacked, TOK)
            result = (resid[:, cols].astype(F32) + q_mr[:, cols].astype(F32) * conv).astype(BF16)
            mixed[:, cols] = result
            result = result.astype(F32)
            return acc + result * result

        squares_sum = lax.fori_loop(starts[c], starts[c] + CHUNKS[c], mr_tile, squares_sum, unroll=True)

    row_sum = jnp.sum(squares_sum, axis=1, keepdims=True)
    line = jnp.sum(jnp.where(diagonal, row_sum, 0.0), axis=0, keepdims=True)
    squares[tp] = jnp.broadcast_to(line, (8, TOK))
    tp_copies = []
    for d in (2, 1, 3):
        copy = pltpu.make_async_remote_copy(
            src_ref=squares.at[tp],
            dst_ref=squares.at[tp],
            send_sem=tp_send.at[d],
            recv_sem=tp_recv.at[d],
            device_id=(me, (tp + d) % tp_size),
            device_id_type=MESH,
        )
        copy.start()
        tp_copies.append(copy)
    mixed_copy = pltpu.make_async_copy(mixed, mixed_h, out_sem.at[0])
    mixed_copy.start()
    for name in ("k_lr", "gain", "q_lr"):
        in_copies[name].wait()

    gain[...] = gain_in[...].astype(F32)

    def gate_tile(j, carry):
        cols = pl.ds(pl.multiple_of(j * LANES, LANES), LANES)
        scaled = mixed[:, cols].astype(F32) * gain[pl.ds(j, 1), :]
        gated[:, cols] = scaled * k_lr[:, cols].astype(F32)
        return carry

    lax.fori_loop(0, tiles, leave_table, 0, unroll=4)
    lax.fori_loop(0, tiles, gate_tile, 0, unroll=4)
    for copy in tp_copies:
        copy.wait_recv()
    line = squares[0, :1, :]
    for d in range(1, tp_size):
        line = line + squares[d, :1, :]
    line = lax.rsqrt(line / (channels * tp_size) + 1e-06)
    scale = jnp.sum(jnp.where(diagonal, line, 0.0), axis=1, keepdims=True)

    lr_in = window

    for copy in halo:
        @pl.when(jnp.logical_not(last))
        def _():
            copy.wait_send()

    own_copies = []
    for s, (dz, dx) in enumerate(OWNER_STEPS):
        z_to, x_to = (z_at + dz) % 2, (x_at + dx) % 4
        owner = z_to * 4 + x_to
        for half in range(2):
            j = owner * 2 + half
            cols = pl.ds(pl.multiple_of(j * LANES, LANES), LANES)
            value = gated[:, cols] * scale
            high = value.astype(BF16)
            low = (value - high.astype(F32)).astype(BF16)
            lr_in[:TOK, cols] = high
            lr_in[TOK:, cols] = low
            rows = pl.ds(pl.multiple_of(j * LANES, LANES), LANES)
            stacked = jnp.dot(
                leave_tab[rows, :],
                jnp.concatenate([high, high, low], axis=0),
                preferred_element_type=F32,
            )
            states[s, half * POLES : (half + 1) * POLES, :] = own_lanes(stacked, POLES).astype(BF16)
        copy = pltpu.make_async_remote_copy(
            src_ref=states.at[s],
            dst_ref=gathered.at[member],
            send_sem=own_send.at[s],
            recv_sem=own_recv,
            device_id=(
                jnp.where(is_owner & ((dz, dx) == (0, 0)), me - 1, base + z_to * 8 + x_to * 2 + 1),
                tp,
            ),
            device_id_type=MESH,
        )
        own_copies.append(copy)
        if (dz, dx) == (0, 0):
            @pl.when(is_owner)
            def _():
                gathered[member] = states[s]

            @pl.when(jnp.logical_not(is_owner))
            def _():
                copy.start()
        else:
            copy.start()

    def lr_conv_tile(j, carry):
        cols = pl.ds(pl.multiple_of(j * LANES, LANES), LANES)
        rows = pl.ds(pl.multiple_of(j * PER_TILE * TOK, TOK), PER_TILE * TOK)
        high, low = lr_in[:TOK, cols], lr_in[TOK:, cols]
        stacked = jnp.dot(
            lr_tab[rows, :], jnp.concatenate([high, high, low], axis=0), preferred_element_type=F32
        )
        local[:, cols] = own_lanes(stacked, TOK)
        return carry

    lax.fori_loop(0, tiles, lr_tables, 0, unroll=4)

    hear(2)

    my_owner = z_at * 4 + x_at

    def total_copy(d, to):
        return pltpu.make_async_remote_copy(
            src_ref=total,
            dst_ref=totals.at[block],
            send_sem=tot_send.at[d],
            recv_sem=tot_recv.at[block],
            device_id=(to * BLOCK + member, tp),
            device_id_type=MESH,
        )

    back_steps = [(dz, dx, c) for dz, dx in OWNER_STEPS for c in (0, 1)]
    back_steps.remove((0, 0, 1))

    @pl.when(is_owner)
    def _():
        lane = lax.broadcasted_iota(jnp.int32, (LANES, 2 * LANES), 1)
        row = lax.broadcasted_iota(jnp.int32, (LANES, 2 * LANES), 0)
        spread = (row == my_owner * 2 * PER_TILE + lane // GROUP).astype(F32)
        wide_rate = jnp.dot(
            rate[...], spread, precision=lax.Precision.HIGHEST, preferred_element_type=F32
        )
        wide_rate = jnp.concatenate([wide_rate[:, :LANES], wide_rate[:, LANES:]], axis=0)
        through = jnp.exp(-wide_rate * TOK)
        through_block = jnp.exp(-wide_rate * (TOK * BLOCK))
        pltpu.make_async_copy(
            gathered.at[pl.ds(0, BLOCK - 1)], gathered.at[pl.ds(0, BLOCK - 1)], own_recv
        ).wait()
        state = jnp.zeros((2 * POLES, LANES), F32)
        for i in range(BLOCK):
            state = state * through + gathered[i].astype(F32)
        total[...] = state.astype(BF16)
        for d in BLOCK_STEPS:
            @pl.when(block + d < blocks)
            def _():
                total_copy(d, block + d).start()

        lax.fori_loop(0, tiles, lr_conv_tile, 0, unroll=4)
        lax.fori_loop(0, tiles, entry_table, 0, unroll=4)

        carried = jnp.zeros((2 * POLES, LANES), F32)
        for b in range(blocks - 1):
            @pl.when(b < block)
            def _():
                pltpu.make_async_copy(totals.at[b], totals.at[b], tot_recv.at[b]).wait()

        for b in range(blocks - 1):
            carried = jnp.where(b < block, carried * through_block + totals[b].astype(F32), carried)
        for i in range(BLOCK):
            carry_out[i] = carried.astype(BF16)
            if i < BLOCK - 1:
                carried = carried * through + gathered[i].astype(F32)
        for s, (dz, dx, c) in enumerate(back_steps):
            to = ((z_at + dz) % 2) * 8 + ((x_at + dx) % 4) * 2 + c
            pltpu.make_async_remote_copy(
                src_ref=carry_out.at[to],
                dst_ref=carry_in.at[my_owner],
                send_sem=back_send.at[s],
                recv_sem=back_recv.at[my_owner],
                device_id=(base + to, tp),
                device_id_type=MESH,
            ).start()
        carry_in[my_owner] = carry_out[member]

    @pl.when(jnp.logical_not(is_owner))
    def _():
        lax.fori_loop(0, tiles, lr_conv_tile, 0, unroll=4)
        lax.fori_loop(0, tiles, entry_table, 0, unroll=4)

    lane_group = lax.broadcasted_iota(jnp.int32, (POLES, LANES), 1) // GROUP
    pole_masks = [(lane_group == i).astype(F32).astype(BF16) for i in range(PER_TILE)]

    def out_tile(owner, half):
        cols = pl.ds(pl.multiple_of((owner * 2 + half) * LANES, LANES), LANES)
        rows = pl.ds(pl.multiple_of((owner * 2 + half) * TOK, TOK), TOK)
        came = carry_in[owner, half * POLES : (half + 1) * POLES, :]
        spread = [came * mask for mask in pole_masks]
        spread = jnp.concatenate(spread + spread, axis=0)
        incoming = jnp.dot(entry_tab[rows, :], spread, preferred_element_type=F32)
        conv = local[:, cols] + incoming
        lr_out[:, cols] = (q_lr[:, cols].astype(F32) * conv).astype(BF16)

    out_copies = []
    for s, (dz, dx) in enumerate(reversed(OWNER_STEPS)):
        owner = ((z_at + dz) % 2) * 4 + (x_at + dx) % 4

        def arrive():
            pltpu.make_async_copy(carry_in.at[owner], carry_in.at[owner], back_recv.at[owner]).wait()

        if (dz, dx) == (0, 0):
            pl.when(jnp.logical_not(is_owner))(arrive)
        else:
            arrive()
        for half in range(2):
            out_tile(owner, half)
        cols = pl.ds(pl.multiple_of(owner * 2 * LANES, 2 * LANES), 2 * LANES)
        copy = pltpu.make_async_copy(lr_out.at[:, cols], out_h.at[:, cols], out_sem.at[1 + s])
        copy.start()
        out_copies.append(copy)

    for copy in tp_copies:
        copy.wait_send()
    for (dz, dx), copy in zip(OWNER_STEPS, own_copies):
        if (dz, dx) == (0, 0):
            @pl.when(jnp.logical_not(is_owner))
            def _():
                copy.wait_send()
        else:
            copy.wait_send()

    @pl.when(is_owner)
    def _():
        for d in BLOCK_STEPS:
            @pl.when(block + d < blocks)
            def _():
                total_copy(d, block + d).wait_send()
        for s in range(len(back_steps)):
            pltpu.make_async_copy(carry_out.at[0], carry_out.at[0], back_send.at[s]).wait()

    mixed_copy.wait()
    for copy in out_copies:
        copy.wait()


def hand_over(mixed, lr_out, mixed_to, lr_out_to, held, in_sems, out_sems):
    rows = TOK // HAND_PIECES
    inward, outward = [], []
    for c in range(HAND_PIECES):
        part = pl.ds(c * rows, rows)
        for i, (src, dst) in enumerate(((mixed, mixed_to), (lr_out, lr_out_to))):
            inward.append(pltpu.make_async_copy(src.at[part], held.at[i, part], in_sems.at[i, c]))
            outward.append(pltpu.make_async_copy(held.at[i, part], dst.at[part], out_sems.at[i, c]))
    for copy in inward:
        copy.start()
    for came, copy in zip(inward, outward):
        came.wait()
        copy.start()
    for copy in outward:
        copy.wait()


def per_device(resid, q_mr, k_mr, v_mr, mr_taps, norm_gain, q_lr, k_lr, pole_rate, residue):
    tok, channels = resid.shape
    tp_size = lax.axis_size("tp")
    blocks = lax.axis_size("ctx") // BLOCK
    tiles = channels // LANES
    groups = channels // GROUP
    big = pltpu.VMEM((tok, channels), BF16)
    scratch = [
        big, big, big, big, big, big,
        pltpu.VMEM((groups, TOK), BF16),
        pltpu.VMEM((tiles, LANES), F32),
        pltpu.VMEM((tiles, LANES), BF16),
        pltpu.VMEM((POLES, groups), F32),
        pltpu.VMEM((POLES, groups), F32),
        pltpu.VMEM((2 * TOK, channels), BF16),
        pltpu.VMEM((groups * TOK, 2 * TOK), BF16),
        pltpu.VMEM((groups * TOK, 3 * TOK), BF16),
        pltpu.VMEM((groups * POLES, 3 * TOK), BF16),
        pltpu.VMEM((tiles * TOK, 2 * LANES), BF16),
        pltpu.VMEM((groups, TOK), F32),
        pltpu.VMEM((POLES, groups), F32),
        pltpu.VMEM((groups, TOK), F32),
        big,
        pltpu.VMEM((tok, channels), F32),
        pltpu.VMEM((tok, channels), F32),
        big,
        pltpu.VMEM((tp_size, 8, TOK), F32),
        pltpu.VMEM((OWNERS, 2 * POLES, LANES), BF16),
        pltpu.VMEM((BLOCK, 2 * POLES, LANES), BF16),
        pltpu.VMEM((2 * POLES, LANES), BF16),
        pltpu.VMEM((blocks, 2 * POLES, LANES), BF16),
        pltpu.VMEM((BLOCK, 2 * POLES, LANES), BF16),
        pltpu.VMEM((OWNERS, 2 * POLES, LANES), BF16),
        pltpu.SemaphoreType.DMA((2, len(CHUNKS))),
        pltpu.SemaphoreType.DMA((8,)),
        pltpu.SemaphoreType.DMA((1 + OWNERS,)),
        pltpu.SemaphoreType.DMA((len(CHUNKS),)),
        pltpu.SemaphoreType.DMA((len(CHUNKS),)),
        pltpu.SemaphoreType.DMA((tp_size,)),
        pltpu.SemaphoreType.DMA((tp_size,)),
        pltpu.SemaphoreType.DMA((OWNERS,)),
        pltpu.SemaphoreType.DMA,
        pltpu.SemaphoreType.DMA((blocks,)),
        pltpu.SemaphoreType.DMA((blocks,)),
        pltpu.SemaphoreType.DMA((2 * OWNERS,)),
        pltpu.SemaphoreType.DMA((OWNERS,)),
        pltpu.SemaphoreType.REGULAR((2,)),
    ]
    in_place = pl.BlockSpec(memory_space=pl.ANY)
    out = jax.ShapeDtypeStruct((tok, channels), BF16)
    results = pl.pallas_call(
        functools.partial(kernel, blocks, tp_size),
        out_shape=(out, out),
        in_specs=[in_place] * 10,
        out_specs=(in_place, in_place),
        scratch_shapes=scratch,
        compiler_params=pltpu.CompilerParams(
            collective_id=0, has_side_effects=True, vmem_limit_bytes=56 * 1024 * 1024
        ),
        name="mixers",
    )(resid, q_mr, k_mr, v_mr, mr_taps, norm_gain.reshape(tiles, LANES), q_lr, k_lr, pole_rate, residue)
    return pl.pallas_call(
        hand_over,
        out_shape=(out, out),
        in_specs=[in_place] * 2,
        out_specs=(in_place, in_place),
        scratch_shapes=[
            pltpu.VMEM((2, tok, channels), BF16),
            pltpu.SemaphoreType.DMA((2, HAND_PIECES)),
            pltpu.SemaphoreType.DMA((2, HAND_PIECES)),
        ],
        compiler_params=pltpu.CompilerParams(vmem_limit_bytes=56 * 1024 * 1024),
        name="hand_over",
    )(*results)


def solution(mesh):
    placed = (
        P("ctx", "tp"),
        P("ctx", "tp"),
        P("ctx", "tp"),
        P("ctx", "tp"),
        P("tp", None),
        P("tp"),
        P("ctx", "tp"),
        P("ctx", "tp"),
        P(None, "tp"),
        P(None, "tp"),
    )
    return jax.shard_map(
        per_device,
        mesh=mesh,
        in_specs=placed,
        out_specs=(P("ctx", "tp"), P("ctx", "tp")),
        check_vma=False,
    )
```

```python
import functools

import jax
import jax.numpy as jnp
from jax import lax
from jax.experimental import pallas as pl
from jax.experimental.pallas import tpu as pltpu
from jax.sharding import PartitionSpec as P

F32 = jnp.float32
BF16 = jnp.bfloat16
MESH = pl.DeviceIdType.MESH

TOK = 128
LANES = 128
GROUP = 16
PER_TILE = LANES // GROUP
POLES = 16
BLOCK = 16
OWNERS = 8
CHUNKS = (4, 4, 4, 2, 2)

TWO_TP, ROUND_1, ROUND_2, ROUND_3, ALL_OWNERS, BLOCKS_1, BLOCKS_2 = range(7)

HAND_PIECES = 8

OWNER_STEPS = ((1, 2), (0, 2), (1, 1), (1, 3), (0, 1), (0, 3), (1, 0), (0, 0))
BLOCK_STEPS = (4, 3, 5, 2, 6, 1, 7)


def shared_steps(rate, residue):
    y = 2.0 * rate
    series = jnp.ones_like(y)
    for order in range(10, 1, -1):
        series = 1.0 - series * y / order
    gap = jnp.where(y < 0.5, y * series, 1.0 - jnp.exp(-y))
    return residue * jnp.sqrt(gap)


def kernel(
    blocks,
    tp_size,
    resid_h, q_mr_h, k_mr_h, v_mr_h, taps_h, gain_h, q_lr_h, k_lr_h, rate_h, residue_h,
    mixed_h, out_h,
    k_mr, v_mr, resid, q_mr, k_lr, q_lr, taps, gain, gain_in, rate, residue,
    window, mr_tab, lr_tab, leave_tab, entry_tab, taps_rev, weight_eff, impulse,
    mixed, gated, local, lr_out, squares, states, gathered, total, totals, carry_out, carry_in,
    kv_sem, in_sem, out_sem, halo_send, halo_recv, tp_send, tp_recv,
    own_send, own_recv, tot_send, tot_recv, back_send, back_recv, relay,
):
    me = lax.axis_index("ctx")
    tp = lax.axis_index("tp")
    shards = blocks * BLOCK
    channels = k_mr.shape[1]
    tiles = channels // LANES
    starts = [sum(CHUNKS[:c]) for c in range(len(CHUNKS))]
    block = me // BLOCK
    member = me % BLOCK
    base = block * BLOCK
    core = me % 2
    x_at = (me // 2) % 4
    z_at = (me // 8) % 2
    first = me == 0
    last = me == shards - 1
    is_owner = core == 1

    totals[...] = jnp.zeros_like(totals)

    barrier = pltpu.get_barrier_semaphore()

    def greet(ctx, tp_to):
        pl.semaphore_signal(barrier, inc=1, device_id=(ctx, tp_to), device_id_type=MESH)

    @pl.when(jnp.logical_not(last))
    def _():
        greet(me + 1, tp)

    @pl.when(jnp.logical_not(first))
    def _():
        greet(me - 1, tp)

    for d in (1, tp_size - 1):
        greet(me, (tp + d) % tp_size)
    plane = me // 8
    planes = shards // 8
    beside = [plane * 8 + ((x_at + d) % 4) * 2 + core for d in (1, 3)]
    above = [((plane + d) % planes) * 8 + x_at * 2 + core for d in (1, planes - 1)]
    partner = base + (1 - z_at) * 8 + x_at * 2 + core

    @pl.when(is_owner)
    def _():
        for to in beside + above:
            greet(to, tp)

    kv_copies = []
    for c in range(len(CHUNKS)):
        cols = pl.ds(starts[c] * LANES, CHUNKS[c] * LANES)
        pair = []
        for i, (src, dst) in enumerate(((k_mr_h, k_mr), (v_mr_h, v_mr))):
            copy = pltpu.make_async_copy(src.at[:, cols], dst.at[:, cols], kv_sem.at[i, c])
            copy.start()
            pair.append(copy)
        kv_copies.append(pair)
    halo = []
    for c in range(len(CHUNKS)):
        for copy in kv_copies[c]:
            copy.wait()
        cols = pl.ds(starts[c] * LANES, CHUNKS[c] * LANES)
        window[TOK:, cols] = (k_mr[:, cols].astype(F32) * v_mr[:, cols].astype(F32)).astype(BF16)
        if c == 0:
            ends = jnp.where(first, 0, 1) + jnp.where(last, 0, 1)
            near = jnp.where(is_owner, 2 + 4, 2)
            pl.semaphore_wait(barrier, ends + near)

        copy = pltpu.make_async_remote_copy(
            src_ref=window.at[pl.ds(TOK, TOK), cols],
            dst_ref=window.at[pl.ds(0, TOK), cols],
            send_sem=halo_send.at[c],
            recv_sem=halo_recv.at[c],
            device_id=(jnp.where(last, me - 1, me + 1), tp),
            device_id_type=MESH,
        )
        halo.append(copy)

        @pl.when(jnp.logical_not(last))
        def _():
            copy.start()

    @pl.when(first)
    def _():
        window[:TOK, :] = jnp.zeros((TOK, channels), BF16)

    def tell(word, to, to_tp):
        pl.semaphore_signal(
            relay.at[word], inc=1, device_id=(to, to_tp), device_id_type=MESH
        )

    def tell_blocks(word, step):
        for d in (step, blocks - step):
            tell(word, ((block + d) % blocks) * BLOCK + member, tp)

    tell(TWO_TP, me, (tp + 1) % tp_size)

    @pl.when(is_owner)
    def _():
        for to in beside + above:
            tell(ROUND_1, to, tp)

    in_copies = {}
    for i, (name, src, dst) in enumerate((
        ("taps", taps_h, taps), ("rate", rate_h, rate), ("residue", residue_h, residue),
        ("resid", resid_h, resid), ("q_mr", q_mr_h, q_mr), ("k_lr", k_lr_h, k_lr),
        ("gain", gain_h, gain_in), ("q_lr", q_lr_h, q_lr),
    )):
        in_copies[name] = pltpu.make_async_copy(src, dst, in_sem.at[i])
        in_copies[name].start()

    row_of = lax.broadcasted_iota(jnp.int32, (TOK, TOK), 0)
    col_of = lax.broadcasted_iota(jnp.int32, (TOK, TOK), 1)
    diagonal = row_of == col_of
    causal = col_of <= row_of
    for name in ("taps", "rate", "residue"):
        in_copies[name].wait()
    flip = ((row_of + col_of) % TOK == 0).astype(BF16)
    taps_rev[...] = jnp.dot(taps[...], flip, preferred_element_type=F32)
    weight_eff[...] = shared_steps(rate[...], residue[...])

    def mr_tables(j, carry):
        for i in range(PER_TILE):
            g = j * PER_TILE + i
            line = jnp.broadcast_to(taps_rev[pl.ds(g, 1), :], (TOK, TOK))
            square = pltpu.roll(line, 0, 1, stride=1, stride_axis=0)
            rows = pl.ds(pl.multiple_of(g * TOK, TOK), TOK)
            mr_tab[rows, :TOK] = jnp.where(causal, 0.0, square).astype(BF16)
            mr_tab[rows, TOK:] = jnp.where(causal, square, 0.0).astype(BF16)
        return carry

    lax.fori_loop(0, tiles, mr_tables, 0, unroll=4)

    row_group = row_of // POLES
    rates = jnp.concatenate([rate[...]] * PER_TILE, axis=0)
    weights = jnp.concatenate([weight_eff[...]] * PER_TILE, axis=0)
    backward = (TOK - 1 - col_of).astype(F32)
    forward = (col_of + 1).astype(F32)

    def of_rows(j, values):
        here = col_of == row_group + j * PER_TILE
        return jnp.sum(jnp.where(here, values, 0.0), axis=1, keepdims=True)

    def leave_table(j, carry):
        leave = jnp.exp(-of_rows(j, rates) * backward)
        rows = pl.ds(pl.multiple_of(j * TOK, TOK), TOK)
        high = leave.astype(BF16)
        leave_tab[rows, :TOK] = high
        leave_tab[rows, TOK : 2 * TOK] = (leave - high.astype(F32)).astype(BF16)
        leave_tab[rows, 2 * TOK :] = high
        weighted = of_rows(j, weights) * leave
        lines = [
            jnp.sum(weighted[i * POLES : (i + 1) * POLES], axis=0, keepdims=True)
            for i in range(PER_TILE)
        ]
        rows = pl.ds(pl.multiple_of(j * PER_TILE, PER_TILE), PER_TILE)
        impulse[rows, :] = pltpu.roll(jnp.concatenate(lines, axis=0), 1, 1)
        return carry

    def lr_tables(j, carry):
        for i in range(PER_TILE):
            g = j * PER_TILE + i
            line = jnp.broadcast_to(impulse[pl.ds(g, 1), :], (TOK, TOK))
            square = pltpu.roll(line, 0, 1, stride=1, stride_axis=0)
            rows = pl.ds(pl.multiple_of(g * TOK, TOK), TOK)
            square = jnp.where(causal, square, 0.0)
            high = square.astype(BF16)
            lr_tab[rows, :TOK] = high
            lr_tab[rows, TOK : 2 * TOK] = (square - high.astype(F32)).astype(BF16)
            lr_tab[rows, 2 * TOK :] = high
        return carry

    def entry_table(j, carry):
        entry = (of_rows(j, weights) * jnp.exp(-of_rows(j, rates) * forward)).T
        high = entry.astype(BF16)
        rows = pl.ds(pl.multiple_of(j * TOK, TOK), TOK)
        entry_tab[rows, :LANES] = high
        entry_tab[rows, LANES:] = (entry - high.astype(F32)).astype(BF16)
        return carry

    def own_lanes(stacked, rows):
        mask = lax.broadcasted_iota(jnp.int32, (rows, LANES), 1) // GROUP
        out = stacked[:rows]
        for i in range(1, PER_TILE):
            out = jnp.where(mask == i, stacked[i * rows : (i + 1) * rows], out)
        return out

    @pl.when(is_owner)
    def _():
        pl.semaphore_wait(relay.at[ROUND_1], 4)
        for to in beside + [partner]:
            tell(ROUND_2, to, tp)
        tell_blocks(BLOCKS_1, 1)

    squares_sum = jnp.zeros((TOK, LANES), F32)
    for name in ("resid", "q_mr"):
        in_copies[name].wait()
    for c in range(len(CHUNKS)):
        @pl.when(jnp.logical_not(first))
        def _():
            halo[c].wait_recv()

        def mr_tile(j, acc):
            cols = pl.ds(pl.multiple_of(j * LANES, LANES), LANES)
            rows = pl.ds(pl.multiple_of(j * PER_TILE * TOK, TOK), PER_TILE * TOK)
            stacked = jnp.dot(mr_tab[rows, :], window[:, cols], preferred_element_type=F32)
            conv = own_lanes(stacked, TOK)
            result = (resid[:, cols].astype(F32) + q_mr[:, cols].astype(F32) * conv).astype(BF16)
            mixed[:, cols] = result
            result = result.astype(F32)
            return acc + result * result

        if c == 2:
            @pl.when(is_owner)
            def _():
                pl.semaphore_wait(relay.at[ROUND_2], 3)
                for to in beside + [partner]:
                    tell(ROUND_3, to, tp)
                tell(ALL_OWNERS, me - 1, tp)
                pl.semaphore_wait(relay.at[BLOCKS_1], 2)
                tell_blocks(BLOCKS_2, 2)

        squares_sum = lax.fori_loop(starts[c], starts[c] + CHUNKS[c], mr_tile, squares_sum, unroll=True)

    row_sum = jnp.sum(squares_sum, axis=1, keepdims=True)
    line = jnp.sum(jnp.where(diagonal, row_sum, 0.0), axis=0, keepdims=True)
    squares[tp] = jnp.broadcast_to(line, (8, TOK))
    pl.semaphore_wait(relay.at[TWO_TP], 1)
    tp_copies = []
    for d in (2, 1, 3):
        copy = pltpu.make_async_remote_copy(
            src_ref=squares.at[tp],
            dst_ref=squares.at[tp],
            send_sem=tp_send.at[d],
            recv_sem=tp_recv.at[d],
            device_id=(me, (tp + d) % tp_size),
            device_id_type=MESH,
        )
        copy.start()
        tp_copies.append(copy)
    mixed_copy = pltpu.make_async_copy(mixed, mixed_h, out_sem.at[0])
    mixed_copy.start()
    for name in ("k_lr", "gain", "q_lr"):
        in_copies[name].wait()

    gain[...] = gain_in[...].astype(F32)

    def gate_tile(j, carry):
        cols = pl.ds(pl.multiple_of(j * LANES, LANES), LANES)
        scaled = mixed[:, cols].astype(F32) * gain[pl.ds(j, 1), :]
        gated[:, cols] = scaled * k_lr[:, cols].astype(F32)
        return carry

    lax.fori_loop(0, tiles, leave_table, 0, unroll=4)
    lax.fori_loop(0, tiles, gate_tile, 0, unroll=4)
    for copy in tp_copies:
        copy.wait_recv()
    line = squares[0, :1, :]
    for d in range(1, tp_size):
        line = line + squares[d, :1, :]
    line = lax.rsqrt(line / (channels * tp_size) + 1e-06)
    scale = jnp.sum(jnp.where(diagonal, line, 0.0), axis=1, keepdims=True)

    lr_in = window

    for copy in halo:
        @pl.when(jnp.logical_not(last))
        def _():
            copy.wait_send()

    @pl.when(jnp.logical_not(is_owner))
    def _():
        pl.semaphore_wait(relay.at[ALL_OWNERS], 1)

    own_copies = []
    for s, (dz, dx) in enumerate(OWNER_STEPS):
        z_to, x_to = (z_at + dz) % 2, (x_at + dx) % 4
        owner = z_to * 4 + x_to
        for half in range(2):
            j = owner * 2 + half
            cols = pl.ds(pl.multiple_of(j * LANES, LANES), LANES)
            value = gated[:, cols] * scale
            high = value.astype(BF16)
            low = (value - high.astype(F32)).astype(BF16)
            lr_in[:TOK, cols] = high
            lr_in[TOK:, cols] = low
            rows = pl.ds(pl.multiple_of(j * LANES, LANES), LANES)
            stacked = jnp.dot(
                leave_tab[rows, :],
                jnp.concatenate([high, high, low], axis=0),
                preferred_element_type=F32,
            )
            states[s, half * POLES : (half + 1) * POLES, :] = own_lanes(stacked, POLES).astype(BF16)
        copy = pltpu.make_async_remote_copy(
            src_ref=states.at[s],
            dst_ref=gathered.at[member],
            send_sem=own_send.at[s],
            recv_sem=own_recv,
            device_id=(
                jnp.where(is_owner & ((dz, dx) == (0, 0)), me - 1, base + z_to * 8 + x_to * 2 + 1),
                tp,
            ),
            device_id_type=MESH,
        )
        own_copies.append(copy)
        if (dz, dx) == (0, 0):
            @pl.when(is_owner)
            def _():
                gathered[member] = states[s]

            @pl.when(jnp.logical_not(is_owner))
            def _():
                copy.start()
        else:
            copy.start()

    def lr_conv_tile(j, carry):
        cols = pl.ds(pl.multiple_of(j * LANES, LANES), LANES)
        rows = pl.ds(pl.multiple_of(j * PER_TILE * TOK, TOK), PER_TILE * TOK)
        high, low = lr_in[:TOK, cols], lr_in[TOK:, cols]
        stacked = jnp.dot(
            lr_tab[rows, :], jnp.concatenate([high, high, low], axis=0), preferred_element_type=F32
        )
        local[:, cols] = own_lanes(stacked, TOK)
        return carry

    lax.fori_loop(0, tiles, lr_tables, 0, unroll=4)

    @pl.when(is_owner)
    def _():
        pl.semaphore_wait(relay.at[ROUND_3], 3)
        pl.semaphore_wait(relay.at[BLOCKS_2], 2)

    my_owner = z_at * 4 + x_at

    def total_copy(d, to):
        return pltpu.make_async_remote_copy(
            src_ref=total,
            dst_ref=totals.at[block],
            send_sem=tot_send.at[d],
            recv_sem=tot_recv.at[block],
            device_id=(to * BLOCK + member, tp),
            device_id_type=MESH,
        )

    back_steps = [(dz, dx, c) for dz, dx in OWNER_STEPS for c in (0, 1)]
    back_steps.remove((0, 0, 1))

    @pl.when(is_owner)
    def _():
        lane = lax.broadcasted_iota(jnp.int32, (LANES, 2 * LANES), 1)
        row = lax.broadcasted_iota(jnp.int32, (LANES, 2 * LANES), 0)
        spread = (row == my_owner * 2 * PER_TILE + lane // GROUP).astype(F32)
        wide_rate = jnp.dot(
            rate[...], spread, precision=lax.Precision.HIGHEST, preferred_element_type=F32
        )
        wide_rate = jnp.concatenate([wide_rate[:, :LANES], wide_rate[:, LANES:]], axis=0)
        through = jnp.exp(-wide_rate * TOK)
        through_block = jnp.exp(-wide_rate * (TOK * BLOCK))
        pltpu.make_async_copy(
            gathered.at[pl.ds(0, BLOCK - 1)], gathered.at[pl.ds(0, BLOCK - 1)], own_recv
        ).wait()
        state = jnp.zeros((2 * POLES, LANES), F32)
        for i in range(BLOCK):
            state = state * through + gathered[i].astype(F32)
        total[...] = state.astype(BF16)
        for d in BLOCK_STEPS:
            @pl.when(block + d < blocks)
            def _():
                total_copy(d, block + d).start()

        lax.fori_loop(0, tiles, lr_conv_tile, 0, unroll=4)
        lax.fori_loop(0, tiles, entry_table, 0, unroll=4)

        carried = jnp.zeros((2 * POLES, LANES), F32)
        for b in range(blocks - 1):
            @pl.when(b < block)
            def _():
                pltpu.make_async_copy(totals.at[b], totals.at[b], tot_recv.at[b]).wait()

        for b in range(blocks - 1):
            carried = jnp.where(b < block, carried * through_block + totals[b].astype(F32), carried)
        for i in range(BLOCK):
            carry_out[i] = carried.astype(BF16)
            if i < BLOCK - 1:
                carried = carried * through + gathered[i].astype(F32)
        for s, (dz, dx, c) in enumerate(back_steps):
            to = ((z_at + dz) % 2) * 8 + ((x_at + dx) % 4) * 2 + c
            pltpu.make_async_remote_copy(
                src_ref=carry_out.at[to],
                dst_ref=carry_in.at[my_owner],
                send_sem=back_send.at[s],
                recv_sem=back_recv.at[my_owner],
                device_id=(base + to, tp),
                device_id_type=MESH,
            ).start()
        carry_in[my_owner] = carry_out[member]

    @pl.when(jnp.logical_not(is_owner))
    def _():
        lax.fori_loop(0, tiles, lr_conv_tile, 0, unroll=4)
        lax.fori_loop(0, tiles, entry_table, 0, unroll=4)

    lane_group = lax.broadcasted_iota(jnp.int32, (POLES, LANES), 1) // GROUP
    pole_masks = [(lane_group == i).astype(F32).astype(BF16) for i in range(PER_TILE)]

    def out_tile(owner, half):
        cols = pl.ds(pl.multiple_of((owner * 2 + half) * LANES, LANES), LANES)
        rows = pl.ds(pl.multiple_of((owner * 2 + half) * TOK, TOK), TOK)
        came = carry_in[owner, half * POLES : (half + 1) * POLES, :]
        spread = [came * mask for mask in pole_masks]
        spread = jnp.concatenate(spread + spread, axis=0)
        incoming = jnp.dot(entry_tab[rows, :], spread, preferred_element_type=F32)
        conv = local[:, cols] + incoming
        lr_out[:, cols] = (q_lr[:, cols].astype(F32) * conv).astype(BF16)

    out_copies = []
    for s, (dz, dx) in enumerate(reversed(OWNER_STEPS)):
        owner = ((z_at + dz) % 2) * 4 + (x_at + dx) % 4

        def arrive():
            pltpu.make_async_copy(carry_in.at[owner], carry_in.at[owner], back_recv.at[owner]).wait()

        if (dz, dx) == (0, 0):
            pl.when(jnp.logical_not(is_owner))(arrive)
        else:
            arrive()
        for half in range(2):
            out_tile(owner, half)
        cols = pl.ds(pl.multiple_of(owner * 2 * LANES, 2 * LANES), 2 * LANES)
        copy = pltpu.make_async_copy(lr_out.at[:, cols], out_h.at[:, cols], out_sem.at[1 + s])
        copy.start()
        out_copies.append(copy)

    for copy in tp_copies:
        copy.wait_send()
    for (dz, dx), copy in zip(OWNER_STEPS, own_copies):
        if (dz, dx) == (0, 0):
            @pl.when(jnp.logical_not(is_owner))
            def _():
                copy.wait_send()
        else:
            copy.wait_send()

    @pl.when(is_owner)
    def _():
        for d in BLOCK_STEPS:
            @pl.when(block + d < blocks)
            def _():
                total_copy(d, block + d).wait_send()
        for s in range(len(back_steps)):
            pltpu.make_async_copy(carry_out.at[0], carry_out.at[0], back_send.at[s]).wait()

    mixed_copy.wait()
    for copy in out_copies:
        copy.wait()


def hand_over(mixed, lr_out, mixed_to, lr_out_to, held, in_sems, out_sems):
    rows = TOK // HAND_PIECES
    inward, outward = [], []
    for c in range(HAND_PIECES):
        part = pl.ds(c * rows, rows)
        for i, (src, dst) in enumerate(((mixed, mixed_to), (lr_out, lr_out_to))):
            inward.append(pltpu.make_async_copy(src.at[part], held.at[i, part], in_sems.at[i, c]))
            outward.append(pltpu.make_async_copy(held.at[i, part], dst.at[part], out_sems.at[i, c]))
    for copy in inward:
        copy.start()
    for came, copy in zip(inward, outward):
        came.wait()
        copy.start()
    for copy in outward:
        copy.wait()


def per_device(resid, q_mr, k_mr, v_mr, mr_taps, norm_gain, q_lr, k_lr, pole_rate, residue):
    tok, channels = resid.shape
    tp_size = lax.axis_size("tp")
    blocks = lax.axis_size("ctx") // BLOCK
    tiles = channels // LANES
    groups = channels // GROUP
    big = pltpu.VMEM((tok, channels), BF16)
    scratch = [
        big, big, big, big, big, big,
        pltpu.VMEM((groups, TOK), BF16),
        pltpu.VMEM((tiles, LANES), F32),
        pltpu.VMEM((tiles, LANES), BF16),
        pltpu.VMEM((POLES, groups), F32),
        pltpu.VMEM((POLES, groups), F32),
        pltpu.VMEM((2 * TOK, channels), BF16),
        pltpu.VMEM((groups * TOK, 2 * TOK), BF16),
        pltpu.VMEM((groups * TOK, 3 * TOK), BF16),
        pltpu.VMEM((groups * POLES, 3 * TOK), BF16),
        pltpu.VMEM((tiles * TOK, 2 * LANES), BF16),
        pltpu.VMEM((groups, TOK), F32),
        pltpu.VMEM((POLES, groups), F32),
        pltpu.VMEM((groups, TOK), F32),
        big,
        pltpu.VMEM((tok, channels), F32),
        pltpu.VMEM((tok, channels), F32),
        big,
        pltpu.VMEM((tp_size, 8, TOK), F32),
        pltpu.VMEM((OWNERS, 2 * POLES, LANES), BF16),
        pltpu.VMEM((BLOCK, 2 * POLES, LANES), BF16),
        pltpu.VMEM((2 * POLES, LANES), BF16),
        pltpu.VMEM((blocks, 2 * POLES, LANES), BF16),
        pltpu.VMEM((BLOCK, 2 * POLES, LANES), BF16),
        pltpu.VMEM((OWNERS, 2 * POLES, LANES), BF16),
        pltpu.SemaphoreType.DMA((2, len(CHUNKS))),
        pltpu.SemaphoreType.DMA((8,)),
        pltpu.SemaphoreType.DMA((1 + OWNERS,)),
        pltpu.SemaphoreType.DMA((len(CHUNKS),)),
        pltpu.SemaphoreType.DMA((len(CHUNKS),)),
        pltpu.SemaphoreType.DMA((tp_size,)),
        pltpu.SemaphoreType.DMA((tp_size,)),
        pltpu.SemaphoreType.DMA((OWNERS,)),
        pltpu.SemaphoreType.DMA,
        pltpu.SemaphoreType.DMA((blocks,)),
        pltpu.SemaphoreType.DMA((blocks,)),
        pltpu.SemaphoreType.DMA((2 * OWNERS,)),
        pltpu.SemaphoreType.DMA((OWNERS,)),
        pltpu.SemaphoreType.REGULAR((7,)),
    ]
    in_place = pl.BlockSpec(memory_space=pl.ANY)
    out = jax.ShapeDtypeStruct((tok, channels), BF16)
    results = pl.pallas_call(
        functools.partial(kernel, blocks, tp_size),
        out_shape=(out, out),
        in_specs=[in_place] * 10,
        out_specs=(in_place, in_place),
        scratch_shapes=scratch,
        compiler_params=pltpu.CompilerParams(
            collective_id=0, has_side_effects=True, vmem_limit_bytes=56 * 1024 * 1024
        ),
        name="mixers",
    )(resid, q_mr, k_mr, v_mr, mr_taps, norm_gain.reshape(tiles, LANES), q_lr, k_lr, pole_rate, residue)
    return pl.pallas_call(
        hand_over,
        out_shape=(out, out),
        in_specs=[in_place] * 2,
        out_specs=(in_place, in_place),
        scratch_shapes=[
            pltpu.VMEM((2, tok, channels), BF16),
            pltpu.SemaphoreType.DMA((2, HAND_PIECES)),
            pltpu.SemaphoreType.DMA((2, HAND_PIECES)),
        ],
        compiler_params=pltpu.CompilerParams(vmem_limit_bytes=56 * 1024 * 1024),
        name="hand_over",
    )(*results)


def solution(mesh):
    placed = (
        P("ctx", "tp"),
        P("ctx", "tp"),
        P("ctx", "tp"),
        P("ctx", "tp"),
        P("tp", None),
        P("tp"),
        P("ctx", "tp"),
        P("ctx", "tp"),
        P(None, "tp"),
        P(None, "tp"),
    )
    return jax.shard_map(
        per_device,
        mesh=mesh,
        in_specs=placed,
        out_specs=(P("ctx", "tp"), P("ctx", "tp")),
        check_vma=False,
    )
```

```python
import functools

import jax
import jax.numpy as jnp
from jax import lax
from jax.experimental import pallas as pl
from jax.experimental.pallas import tpu as pltpu
from jax.sharding import PartitionSpec as P

F32 = jnp.float32
BF16 = jnp.bfloat16
MESH = pl.DeviceIdType.MESH

TOK = 128
LANES = 128
GROUP = 16
PER_TILE = LANES // GROUP
POLES = 16
BLOCK = 16
OWNERS = 8
CHUNKS = (4, 4, 4, 3, 1)

TWO_TP, ROUND_1, ROUND_2, ROUND_3, ALL_OWNERS, BLOCKS_1, BLOCKS_2, BLOCKS_4 = range(8)

HAND_PIECES = 4

OWNER_STEPS = ((1, 2), (0, 2), (1, 1), (1, 3), (0, 1), (0, 3), (1, 0), (0, 0))
NEAR_BLOCKS = (4, 3, 2, 1)
FAR_BLOCKS = (5, 6, 7)


def shared_steps(rate, residue):
    y = 2.0 * rate
    series = jnp.ones_like(y)
    for order in range(10, 1, -1):
        series = 1.0 - series * y / order
    gap = jnp.where(y < 0.5, y * series, 1.0 - jnp.exp(-y))
    return residue * jnp.sqrt(gap)


def kernel(
    blocks,
    tp_size,
    resid_h, q_mr_h, k_mr_h, v_mr_h, taps_h, gain_h, q_lr_h, k_lr_h, rate_h, residue_h,
    mixed_h, out_h,
    k_mr, v_mr, resid, q_mr, k_lr, q_lr, taps, gain, gain_in, rate, residue,
    window, mr_tab, lr_tab, leave_tab, entry_tab, taps_rev, weight_eff, impulse,
    mixed, gated, local, lr_out, squares, states, gathered, total, totals, carry_out, carry_in,
    kv_sem, in_sem, out_sem, halo_send, halo_recv, tp_send, tp_recv,
    own_send, own_recv, tot_send, tot_recv, back_send, back_recv, relay,
):
    me = lax.axis_index("ctx")
    tp = lax.axis_index("tp")
    shards = blocks * BLOCK
    channels = k_mr.shape[1]
    tiles = channels // LANES
    starts = [sum(CHUNKS[:c]) for c in range(len(CHUNKS))]
    block = me // BLOCK
    member = me % BLOCK
    base = block * BLOCK
    core = me % 2
    x_at = (me // 2) % 4
    z_at = (me // 8) % 2
    first = me == 0
    last = me == shards - 1
    is_owner = core == 1

    totals[...] = jnp.zeros_like(totals)

    barrier = pltpu.get_barrier_semaphore()

    def greet(ctx, tp_to):
        pl.semaphore_signal(barrier, inc=1, device_id=(ctx, tp_to), device_id_type=MESH)

    @pl.when(jnp.logical_not(last))
    def _():
        greet(me + 1, tp)

    @pl.when(jnp.logical_not(first))
    def _():
        greet(me - 1, tp)

    for d in (1, tp_size - 1):
        greet(me, (tp + d) % tp_size)
    plane = me // 8
    planes = shards // 8
    beside = [plane * 8 + ((x_at + d) % 4) * 2 + core for d in (1, 3)]
    above = ((plane + 1 < planes, me + 8), (plane > 0, me - 8))
    n_above = jnp.where(plane + 1 < planes, 1, 0) + jnp.where(plane > 0, 1, 0)
    partner = base + (1 - z_at) * 8 + x_at * 2 + core

    @pl.when(is_owner)
    def _():
        for to in beside:
            greet(to, tp)
        for exists, to in above:
            @pl.when(exists)
            def _():
                greet(to, tp)

    kv_copies = []
    for c in range(len(CHUNKS)):
        cols = pl.ds(starts[c] * LANES, CHUNKS[c] * LANES)
        pair = []
        for i, (src, dst) in enumerate(((k_mr_h, k_mr), (v_mr_h, v_mr))):
            copy = pltpu.make_async_copy(src.at[:, cols], dst.at[:, cols], kv_sem.at[i, c])
            copy.start()
            pair.append(copy)
        kv_copies.append(pair)
    halo = []
    for c in range(len(CHUNKS)):
        for copy in kv_copies[c]:
            copy.wait()
        cols = pl.ds(starts[c] * LANES, CHUNKS[c] * LANES)
        window[TOK:, cols] = (k_mr[:, cols].astype(F32) * v_mr[:, cols].astype(F32)).astype(BF16)
        if c == 0:
            ends = jnp.where(first, 0, 1) + jnp.where(last, 0, 1)
            near = jnp.where(is_owner, 2 + 2 + n_above, 2)
            pl.semaphore_wait(barrier, ends + near)

        copy = pltpu.make_async_remote_copy(
            src_ref=window.at[pl.ds(TOK, TOK), cols],
            dst_ref=window.at[pl.ds(0, TOK), cols],
            send_sem=halo_send.at[c],
            recv_sem=halo_recv.at[c],
            device_id=(jnp.where(last, me - 1, me + 1), tp),
            device_id_type=MESH,
        )
        halo.append(copy)

        @pl.when(jnp.logical_not(last))
        def _():
            copy.start()

    @pl.when(first)
    def _():
        window[:TOK, :] = jnp.zeros((TOK, channels), BF16)

    def tell(word, to, to_tp):
        pl.semaphore_signal(
            relay.at[word], inc=1, device_id=(to, to_tp), device_id_type=MESH
        )

    def blocks_at(step):
        return ((block + step < blocks, step), (block >= step, -step))

    def tell_blocks(word, step):
        for exists, d in blocks_at(step):
            @pl.when(exists)
            def _():
                tell(word, me + d * BLOCK, tp)

    def hear_blocks(word, step):
        up, down = blocks_at(step)
        pl.semaphore_wait(relay.at[word], jnp.where(up[0], 1, 0) + jnp.where(down[0], 1, 0))

    tell(TWO_TP, me, (tp + 1) % tp_size)

    @pl.when(is_owner)
    def _():
        for to in beside:
            tell(ROUND_1, to, tp)
        for exists, to in above:
            @pl.when(exists)
            def _():
                tell(ROUND_1, to, tp)

    in_copies = {}
    for i, (name, src, dst) in enumerate((
        ("taps", taps_h, taps), ("rate", rate_h, rate), ("residue", residue_h, residue),
        ("resid", resid_h, resid), ("q_mr", q_mr_h, q_mr), ("k_lr", k_lr_h, k_lr),
        ("gain", gain_h, gain_in), ("q_lr", q_lr_h, q_lr),
    )):
        in_copies[name] = pltpu.make_async_copy(src, dst, in_sem.at[i])
        in_copies[name].start()

    row_of = lax.broadcasted_iota(jnp.int32, (TOK, TOK), 0)
    col_of = lax.broadcasted_iota(jnp.int32, (TOK, TOK), 1)
    diagonal = row_of == col_of
    causal = col_of <= row_of
    for name in ("taps", "rate", "residue"):
        in_copies[name].wait()
    flip = ((row_of + col_of) % TOK == 0).astype(BF16)
    taps_rev[...] = jnp.dot(taps[...], flip, preferred_element_type=F32)
    weight_eff[...] = shared_steps(rate[...], residue[...])

    def mr_tables(j, carry):
        for i in range(PER_TILE):
            g = j * PER_TILE + i
            line = jnp.broadcast_to(taps_rev[pl.ds(g, 1), :], (TOK, TOK))
            square = pltpu.roll(line, 0, 1, stride=1, stride_axis=0)
            rows = pl.ds(pl.multiple_of(g * TOK, TOK), TOK)
            mr_tab[rows, :TOK] = jnp.where(causal, 0.0, square).astype(BF16)
            mr_tab[rows, TOK:] = jnp.where(causal, square, 0.0).astype(BF16)
        return carry

    lax.fori_loop(0, tiles, mr_tables, 0, unroll=4)

    row_group = row_of // POLES
    rates = jnp.concatenate([rate[...]] * PER_TILE, axis=0)
    weights = jnp.concatenate([weight_eff[...]] * PER_TILE, axis=0)
    backward = (TOK - 1 - col_of).astype(F32)
    forward = (col_of + 1).astype(F32)

    def of_rows(j, values):
        here = col_of == row_group + j * PER_TILE
        return jnp.sum(jnp.where(here, values, 0.0), axis=1, keepdims=True)

    def leave_table(j, carry):
        leave = jnp.exp(-of_rows(j, rates) * backward)
        rows = pl.ds(pl.multiple_of(j * TOK, TOK), TOK)
        high = leave.astype(BF16)
        leave_tab[rows, :TOK] = high
        leave_tab[rows, TOK : 2 * TOK] = (leave - high.astype(F32)).astype(BF16)
        leave_tab[rows, 2 * TOK :] = high
        weighted = of_rows(j, weights) * leave
        lines = [
            jnp.sum(weighted[i * POLES : (i + 1) * POLES], axis=0, keepdims=True)
            for i in range(PER_TILE)
        ]
        rows = pl.ds(pl.multiple_of(j * PER_TILE, PER_TILE), PER_TILE)
        impulse[rows, :] = pltpu.roll(jnp.concatenate(lines, axis=0), 1, 1)
        return carry

    def lr_tables(j, carry):
        for i in range(PER_TILE):
            g = j * PER_TILE + i
            line = jnp.broadcast_to(impulse[pl.ds(g, 1), :], (TOK, TOK))
            square = pltpu.roll(line, 0, 1, stride=1, stride_axis=0)
            rows = pl.ds(pl.multiple_of(g * TOK, TOK), TOK)
            square = jnp.where(causal, square, 0.0)
            high = square.astype(BF16)
            lr_tab[rows, :TOK] = high
            lr_tab[rows, TOK : 2 * TOK] = (square - high.astype(F32)).astype(BF16)
            lr_tab[rows, 2 * TOK :] = high
        return carry

    def entry_table(j, carry):
        entry = (of_rows(j, weights) * jnp.exp(-of_rows(j, rates) * forward)).T
        high = entry.astype(BF16)
        rows = pl.ds(pl.multiple_of(j * TOK, TOK), TOK)
        entry_tab[rows, :LANES] = high
        entry_tab[rows, LANES:] = (entry - high.astype(F32)).astype(BF16)
        return carry

    def own_lanes(stacked, rows):
        mask = lax.broadcasted_iota(jnp.int32, (rows, LANES), 1) // GROUP
        out = stacked[:rows]
        for i in range(1, PER_TILE):
            out = jnp.where(mask == i, stacked[i * rows : (i + 1) * rows], out)
        return out


    squares_sum = jnp.zeros((TOK, LANES), F32)
    for name in ("resid", "q_mr"):
        in_copies[name].wait()
    for c in range(len(CHUNKS)):
        @pl.when(jnp.logical_not(first))
        def _():
            halo[c].wait_recv()

        def mr_tile(j, acc):
            cols = pl.ds(pl.multiple_of(j * LANES, LANES), LANES)
            rows = pl.ds(pl.multiple_of(j * PER_TILE * TOK, TOK), PER_TILE * TOK)
            stacked = jnp.dot(mr_tab[rows, :], window[:, cols], preferred_element_type=F32)
            conv = own_lanes(stacked, TOK)
            result = (resid[:, cols].astype(F32) + q_mr[:, cols].astype(F32) * conv).astype(BF16)
            mixed[:, cols] = result
            result = result.astype(F32)
            return acc + result * result

        if c == 1:
            @pl.when(is_owner)
            def _():
                pl.semaphore_wait(relay.at[ROUND_1], 2 + n_above)
                for to in beside + [partner]:
                    tell(ROUND_2, to, tp)
                tell_blocks(BLOCKS_1, 1)

        if c == 3:
            @pl.when(is_owner)
            def _():
                pl.semaphore_wait(relay.at[ROUND_2], 3)
                for to in beside + [partner]:
                    tell(ROUND_3, to, tp)
                tell(ALL_OWNERS, me - 1, tp)

        squares_sum = lax.fori_loop(starts[c], starts[c] + CHUNKS[c], mr_tile, squares_sum, unroll=True)

    row_sum = jnp.sum(squares_sum, axis=1, keepdims=True)
    line = jnp.sum(jnp.where(diagonal, row_sum, 0.0), axis=0, keepdims=True)
    squares[tp] = jnp.broadcast_to(line, (8, TOK))
    pl.semaphore_wait(relay.at[TWO_TP], 1)
    tp_copies = []
    for d in (2, 1, 3):
        copy = pltpu.make_async_remote_copy(
            src_ref=squares.at[tp],
            dst_ref=squares.at[tp],
            send_sem=tp_send.at[d],
            recv_sem=tp_recv.at[d],
            device_id=(me, (tp + d) % tp_size),
            device_id_type=MESH,
        )
        copy.start()
        tp_copies.append(copy)
    mixed_copy = pltpu.make_async_copy(mixed, mixed_h, out_sem.at[0])
    mixed_copy.start()
    for name in ("k_lr", "gain", "q_lr"):
        in_copies[name].wait()

    gain[...] = gain_in[...].astype(F32)

    def gate_tile(j, carry):
        cols = pl.ds(pl.multiple_of(j * LANES, LANES), LANES)
        scaled = mixed[:, cols].astype(F32) * gain[pl.ds(j, 1), :]
        gated[:, cols] = scaled * k_lr[:, cols].astype(F32)
        return carry

    lax.fori_loop(0, tiles, leave_table, 0, unroll=4)
    lax.fori_loop(0, tiles, gate_tile, 0, unroll=4)

    @pl.when(is_owner)
    def _():
        hear_blocks(BLOCKS_1, 1)
        tell_blocks(BLOCKS_2, 2)

    for copy in tp_copies:
        copy.wait_recv()
    line = squares[0, :1, :]
    for d in range(1, tp_size):
        line = line + squares[d, :1, :]
    line = lax.rsqrt(line / (channels * tp_size) + 1e-06)
    scale = jnp.sum(jnp.where(diagonal, line, 0.0), axis=1, keepdims=True)

    lr_in = window

    for copy in halo:
        @pl.when(jnp.logical_not(last))
        def _():
            copy.wait_send()

    @pl.when(jnp.logical_not(is_owner))
    def _():
        pl.semaphore_wait(relay.at[ALL_OWNERS], 1)

    own_copies = []
    for s, (dz, dx) in enumerate(OWNER_STEPS):
        z_to, x_to = (z_at + dz) % 2, (x_at + dx) % 4
        owner = z_to * 4 + x_to
        for half in range(2):
            j = owner * 2 + half
            cols = pl.ds(pl.multiple_of(j * LANES, LANES), LANES)
            value = gated[:, cols] * scale
            high = value.astype(BF16)
            low = (value - high.astype(F32)).astype(BF16)
            lr_in[:TOK, cols] = high
            lr_in[TOK:, cols] = low
            rows = pl.ds(pl.multiple_of(j * LANES, LANES), LANES)
            stacked = jnp.dot(
                leave_tab[rows, :],
                jnp.concatenate([high, high, low], axis=0),
                preferred_element_type=F32,
            )
            states[s, half * POLES : (half + 1) * POLES, :] = own_lanes(stacked, POLES).astype(BF16)
        copy = pltpu.make_async_remote_copy(
            src_ref=states.at[s],
            dst_ref=gathered.at[member],
            send_sem=own_send.at[s],
            recv_sem=own_recv,
            device_id=(
                jnp.where(is_owner & ((dz, dx) == (0, 0)), me - 1, base + z_to * 8 + x_to * 2 + 1),
                tp,
            ),
            device_id_type=MESH,
        )
        own_copies.append(copy)
        if (dz, dx) == (0, 0):
            @pl.when(is_owner)
            def _():
                gathered[member] = states[s]

            @pl.when(jnp.logical_not(is_owner))
            def _():
                copy.start()
        else:
            copy.start()

    far = 4
    passes_far = is_owner & (block >= far) & (block < blocks - 1)

    @pl.when(passes_far)
    def _():
        hear_blocks(BLOCKS_2, 2)
        tell(BLOCKS_4, me - far * BLOCK, tp)

    def lr_conv_tile(j, carry):
        cols = pl.ds(pl.multiple_of(j * LANES, LANES), LANES)
        rows = pl.ds(pl.multiple_of(j * PER_TILE * TOK, TOK), PER_TILE * TOK)
        high, low = lr_in[:TOK, cols], lr_in[TOK:, cols]
        stacked = jnp.dot(
            lr_tab[rows, :], jnp.concatenate([high, high, low], axis=0), preferred_element_type=F32
        )
        local[:, cols] = own_lanes(stacked, TOK)
        return carry

    lax.fori_loop(0, tiles, lr_tables, 0, unroll=4)

    @pl.when(is_owner)
    def _():
        pl.semaphore_wait(relay.at[ROUND_3], 3)

    my_owner = z_at * 4 + x_at

    def total_copy(d, to):
        return pltpu.make_async_remote_copy(
            src_ref=total,
            dst_ref=totals.at[block],
            send_sem=tot_send.at[d],
            recv_sem=tot_recv.at[block],
            device_id=(to * BLOCK + member, tp),
            device_id_type=MESH,
        )

    back_steps = [(dz, dx, c) for dz, dx in OWNER_STEPS for c in (0, 1)]
    back_steps.remove((0, 0, 1))

    @pl.when(is_owner)
    def _():
        lane = lax.broadcasted_iota(jnp.int32, (LANES, 2 * LANES), 1)
        row = lax.broadcasted_iota(jnp.int32, (LANES, 2 * LANES), 0)
        spread = (row == my_owner * 2 * PER_TILE + lane // GROUP).astype(F32)
        wide_rate = jnp.dot(
            rate[...], spread, precision=lax.Precision.HIGHEST, preferred_element_type=F32
        )
        wide_rate = jnp.concatenate([wide_rate[:, :LANES], wide_rate[:, LANES:]], axis=0)
        through = jnp.exp(-wide_rate * TOK)
        through_block = jnp.exp(-wide_rate * (TOK * BLOCK))
        pltpu.make_async_copy(
            gathered.at[pl.ds(0, BLOCK - 1)], gathered.at[pl.ds(0, BLOCK - 1)], own_recv
        ).wait()
        state = jnp.zeros((2 * POLES, LANES), F32)
        for i in range(BLOCK):
            state = state * through + gathered[i].astype(F32)
        total[...] = state.astype(BF16)

        @pl.when(block < far)
        def _():
            hear_blocks(BLOCKS_2, 2)

        for d in NEAR_BLOCKS:
            @pl.when(block + d < blocks)
            def _():
                total_copy(d, block + d).start()

        lax.fori_loop(0, tiles // 2, lr_conv_tile, 0, unroll=4)

        @pl.when(block + far + 1 < blocks)
        def _():
            pl.semaphore_wait(relay.at[BLOCKS_4], 1)

        for d in FAR_BLOCKS:
            @pl.when(block + d < blocks)
            def _():
                total_copy(d, block + d).start()

        lax.fori_loop(tiles // 2, tiles, lr_conv_tile, 0, unroll=4)

        carried = jnp.zeros((2 * POLES, LANES), F32)
        for b in range(blocks - 1):
            @pl.when(b < block)
            def _():
                pltpu.make_async_copy(totals.at[b], totals.at[b], tot_recv.at[b]).wait()

        for b in range(blocks - 1):
            carried = jnp.where(b < block, carried * through_block + totals[b].astype(F32), carried)
        for i in range(BLOCK):
            carry_out[i] = carried.astype(BF16)
            if i < BLOCK - 1:
                carried = carried * through + gathered[i].astype(F32)
        for s, (dz, dx, c) in enumerate(back_steps):
            to = ((z_at + dz) % 2) * 8 + ((x_at + dx) % 4) * 2 + c
            pltpu.make_async_remote_copy(
                src_ref=carry_out.at[to],
                dst_ref=carry_in.at[my_owner],
                send_sem=back_send.at[s],
                recv_sem=back_recv.at[my_owner],
                device_id=(base + to, tp),
                device_id_type=MESH,
            ).start()
        carry_in[my_owner] = carry_out[member]
        lax.fori_loop(0, tiles, entry_table, 0, unroll=4)

    @pl.when(jnp.logical_not(is_owner))
    def _():
        lax.fori_loop(0, tiles, lr_conv_tile, 0, unroll=4)
        lax.fori_loop(0, tiles, entry_table, 0, unroll=4)

    lane_group = lax.broadcasted_iota(jnp.int32, (POLES, LANES), 1) // GROUP
    pole_masks = [(lane_group == i).astype(F32).astype(BF16) for i in range(PER_TILE)]

    def out_tile(owner, half):
        cols = pl.ds(pl.multiple_of((owner * 2 + half) * LANES, LANES), LANES)
        rows = pl.ds(pl.multiple_of((owner * 2 + half) * TOK, TOK), TOK)
        came = carry_in[owner, half * POLES : (half + 1) * POLES, :]
        spread = [came * mask for mask in pole_masks]
        spread = jnp.concatenate(spread + spread, axis=0)
        incoming = jnp.dot(entry_tab[rows, :], spread, preferred_element_type=F32)
        conv = local[:, cols] + incoming
        lr_out[:, cols] = (q_lr[:, cols].astype(F32) * conv).astype(BF16)

    out_copies = []
    for s, (dz, dx) in enumerate(reversed(OWNER_STEPS)):
        owner = ((z_at + dz) % 2) * 4 + (x_at + dx) % 4

        def arrive():
            pltpu.make_async_copy(carry_in.at[owner], carry_in.at[owner], back_recv.at[owner]).wait()

        if (dz, dx) == (0, 0):
            pl.when(jnp.logical_not(is_owner))(arrive)
        else:
            arrive()
        for half in range(2):
            out_tile(owner, half)
        cols = pl.ds(pl.multiple_of(owner * 2 * LANES, 2 * LANES), 2 * LANES)
        copy = pltpu.make_async_copy(lr_out.at[:, cols], out_h.at[:, cols], out_sem.at[1 + s])
        copy.start()
        out_copies.append(copy)

    for copy in tp_copies:
        copy.wait_send()
    for (dz, dx), copy in zip(OWNER_STEPS, own_copies):
        if (dz, dx) == (0, 0):
            @pl.when(jnp.logical_not(is_owner))
            def _():
                copy.wait_send()
        else:
            copy.wait_send()

    @pl.when(is_owner)
    def _():
        @pl.when(block == blocks - 1)
        def _():
            hear_blocks(BLOCKS_2, 2)

        for d in NEAR_BLOCKS + FAR_BLOCKS:
            @pl.when(block + d < blocks)
            def _():
                total_copy(d, block + d).wait_send()
        for s in range(len(back_steps)):
            pltpu.make_async_copy(carry_out.at[0], carry_out.at[0], back_send.at[s]).wait()

    mixed_copy.wait()
    for copy in out_copies:
        copy.wait()


def hand_over(mixed, lr_out, mixed_to, lr_out_to, held, in_sems, out_sems):
    rows = TOK // HAND_PIECES
    inward, outward = [], []
    for c in range(HAND_PIECES):
        part = pl.ds(c * rows, rows)
        for i, (src, dst) in enumerate(((mixed, mixed_to), (lr_out, lr_out_to))):
            inward.append(pltpu.make_async_copy(src.at[part], held.at[i, part], in_sems.at[i, c]))
            outward.append(pltpu.make_async_copy(held.at[i, part], dst.at[part], out_sems.at[i, c]))
    for copy in inward:
        copy.start()
    for came, copy in zip(inward, outward):
        came.wait()
        copy.start()
    for copy in outward:
        copy.wait()


def per_device(resid, q_mr, k_mr, v_mr, mr_taps, norm_gain, q_lr, k_lr, pole_rate, residue):
    tok, channels = resid.shape
    tp_size = lax.axis_size("tp")
    blocks = lax.axis_size("ctx") // BLOCK
    tiles = channels // LANES
    groups = channels // GROUP
    big = pltpu.VMEM((tok, channels), BF16)
    scratch = [
        big, big, big, big, big, big,
        pltpu.VMEM((groups, TOK), BF16),
        pltpu.VMEM((tiles, LANES), F32),
        pltpu.VMEM((tiles, LANES), BF16),
        pltpu.VMEM((POLES, groups), F32),
        pltpu.VMEM((POLES, groups), F32),
        pltpu.VMEM((2 * TOK, channels), BF16),
        pltpu.VMEM((groups * TOK, 2 * TOK), BF16),
        pltpu.VMEM((groups * TOK, 3 * TOK), BF16),
        pltpu.VMEM((groups * POLES, 3 * TOK), BF16),
        pltpu.VMEM((tiles * TOK, 2 * LANES), BF16),
        pltpu.VMEM((groups, TOK), F32),
        pltpu.VMEM((POLES, groups), F32),
        pltpu.VMEM((groups, TOK), F32),
        big,
        pltpu.VMEM((tok, channels), F32),
        pltpu.VMEM((tok, channels), F32),
        big,
        pltpu.VMEM((tp_size, 8, TOK), F32),
        pltpu.VMEM((OWNERS, 2 * POLES, LANES), BF16),
        pltpu.VMEM((BLOCK, 2 * POLES, LANES), BF16),
        pltpu.VMEM((2 * POLES, LANES), BF16),
        pltpu.VMEM((blocks, 2 * POLES, LANES), BF16),
        pltpu.VMEM((BLOCK, 2 * POLES, LANES), BF16),
        pltpu.VMEM((OWNERS, 2 * POLES, LANES), BF16),
        pltpu.SemaphoreType.DMA((2, len(CHUNKS))),
        pltpu.SemaphoreType.DMA((8,)),
        pltpu.SemaphoreType.DMA((1 + OWNERS,)),
        pltpu.SemaphoreType.DMA((len(CHUNKS),)),
        pltpu.SemaphoreType.DMA((len(CHUNKS),)),
        pltpu.SemaphoreType.DMA((tp_size,)),
        pltpu.SemaphoreType.DMA((tp_size,)),
        pltpu.SemaphoreType.DMA((OWNERS,)),
        pltpu.SemaphoreType.DMA,
        pltpu.SemaphoreType.DMA((blocks,)),
        pltpu.SemaphoreType.DMA((blocks,)),
        pltpu.SemaphoreType.DMA((2 * OWNERS,)),
        pltpu.SemaphoreType.DMA((OWNERS,)),
        pltpu.SemaphoreType.REGULAR((8,)),
    ]
    in_place = pl.BlockSpec(memory_space=pl.ANY)
    out = jax.ShapeDtypeStruct((tok, channels), BF16)
    results = pl.pallas_call(
        functools.partial(kernel, blocks, tp_size),
        out_shape=(out, out),
        in_specs=[in_place] * 10,
        out_specs=(in_place, in_place),
        scratch_shapes=scratch,
        compiler_params=pltpu.CompilerParams(
            collective_id=0, has_side_effects=True, vmem_limit_bytes=56 * 1024 * 1024
        ),
        name="mixers",
    )(resid, q_mr, k_mr, v_mr, mr_taps, norm_gain.reshape(tiles, LANES), q_lr, k_lr, pole_rate, residue)
    return pl.pallas_call(
        hand_over,
        out_shape=(out, out),
        in_specs=[in_place] * 2,
        out_specs=(in_place, in_place),
        scratch_shapes=[
            pltpu.VMEM((2, tok, channels), BF16),
            pltpu.SemaphoreType.DMA((2, HAND_PIECES)),
            pltpu.SemaphoreType.DMA((2, HAND_PIECES)),
        ],
        compiler_params=pltpu.CompilerParams(vmem_limit_bytes=56 * 1024 * 1024),
        name="hand_over",
    )(*results)


def solution(mesh):
    placed = (
        P("ctx", "tp"),
        P("ctx", "tp"),
        P("ctx", "tp"),
        P("ctx", "tp"),
        P("tp", None),
        P("tp"),
        P("ctx", "tp"),
        P("ctx", "tp"),
        P(None, "tp"),
        P(None, "tp"),
    )
    return jax.shard_map(
        per_device,
        mesh=mesh,
        in_specs=placed,
        out_specs=(P("ctx", "tp"), P("ctx", "tp")),
        check_vma=False,
    )
```

```python
import functools

import jax
import jax.numpy as jnp
from jax import lax
from jax.experimental import pallas as pl
from jax.experimental.pallas import tpu as pltpu
from jax.sharding import PartitionSpec as P

F32 = jnp.float32
BF16 = jnp.bfloat16
MESH = pl.DeviceIdType.MESH

TOK = 128
LANES = 128
GROUP = 16
PER_TILE = LANES // GROUP
POLES = 16
BLOCK = 16
OWNERS = 8
CHUNKS = (4, 4, 4, 3, 1)

TWO_TP, ROUND_1, ROUND_2, ROUND_3, ALL_OWNERS, BLOCKS_1, BLOCKS_2, BLOCKS_4 = range(8)

HAND_PIECES = 4

OWNER_STEPS = ((1, 2), (0, 2), (1, 1), (1, 3), (0, 1), (0, 3), (1, 0), (0, 0))
NEAR_BLOCKS = (4, 3, 2, 1)
FAR_BLOCKS = (5, 6, 7)


def shared_steps(rate, residue):
    y = 2.0 * rate
    series = jnp.ones_like(y)
    for order in range(10, 1, -1):
        series = 1.0 - series * y / order
    gap = jnp.where(y < 0.5, y * series, 1.0 - jnp.exp(-y))
    return residue * jnp.sqrt(gap)


def kernel(
    blocks,
    tp_size,
    resid_h, q_mr_h, k_mr_h, v_mr_h, taps_h, gain_h, q_lr_h, k_lr_h, rate_h, residue_h,
    mixed_h, out_h,
    k_mr, v_mr, resid, q_mr, k_lr, q_lr, taps, gain, gain_in, rate, residue,
    window, mr_tab, lr_tab, leave_tab, entry_tab, taps_rev, weight_eff, impulse,
    mixed, gated, local, lr_out, squares, states, gathered, total, totals, carry_out, carry_in,
    kv_sem, in_sem, out_sem, halo_send, halo_recv, tp_send, tp_recv,
    own_send, own_recv, tot_send, tot_recv, back_send, back_recv, relay,
):
    me = lax.axis_index("ctx")
    tp = lax.axis_index("tp")
    shards = blocks * BLOCK
    channels = k_mr.shape[1]
    tiles = channels // LANES
    starts = [sum(CHUNKS[:c]) for c in range(len(CHUNKS))]
    block = me // BLOCK
    member = me % BLOCK
    base = block * BLOCK
    core = me % 2
    x_at = (me // 2) % 4
    z_at = (me // 8) % 2
    first = me == 0
    last = me == shards - 1
    is_owner = core == 1

    totals[...] = jnp.zeros_like(totals)

    barrier = pltpu.get_barrier_semaphore()

    def greet(ctx, tp_to):
        pl.semaphore_signal(barrier, inc=1, device_id=(ctx, tp_to), device_id_type=MESH)

    @pl.when(jnp.logical_not(last))
    def _():
        greet(me + 1, tp)

    @pl.when(jnp.logical_not(first))
    def _():
        greet(me - 1, tp)

    for d in (1, tp_size - 1):
        greet(me, (tp + d) % tp_size)
    plane = me // 8
    planes = shards // 8
    beside = [plane * 8 + ((x_at + d) % 4) * 2 + core for d in (1, 3)]
    above = ((plane + 1 < planes, me + 8), (plane > 0, me - 8))
    n_above = jnp.where(plane + 1 < planes, 1, 0) + jnp.where(plane > 0, 1, 0)
    partner = base + (1 - z_at) * 8 + x_at * 2 + core

    @pl.when(is_owner)
    def _():
        for to in beside:
            greet(to, tp)
        for exists, to in above:
            @pl.when(exists)
            def _():
                greet(to, tp)

    kv_copies = []
    for c in range(len(CHUNKS)):
        cols = pl.ds(starts[c] * LANES, CHUNKS[c] * LANES)
        pair = []
        for i, (src, dst) in enumerate(((k_mr_h, k_mr), (v_mr_h, v_mr))):
            copy = pltpu.make_async_copy(src.at[:, cols], dst.at[:, cols], kv_sem.at[i, c])
            copy.start()
            pair.append(copy)
        kv_copies.append(pair)
    halo = []
    for c in range(len(CHUNKS)):
        for copy in kv_copies[c]:
            copy.wait()
        cols = pl.ds(starts[c] * LANES, CHUNKS[c] * LANES)
        window[TOK:, cols] = (k_mr[:, cols].astype(F32) * v_mr[:, cols].astype(F32)).astype(BF16)
        if c == 0:
            ends = jnp.where(first, 0, 1) + jnp.where(last, 0, 1)
            near = jnp.where(is_owner, 2 + 2 + n_above, 2)
            pl.semaphore_wait(barrier, ends + near)

        copy = pltpu.make_async_remote_copy(
            src_ref=window.at[pl.ds(TOK, TOK), cols],
            dst_ref=window.at[pl.ds(0, TOK), cols],
            send_sem=halo_send.at[c],
            recv_sem=halo_recv.at[c],
            device_id=(jnp.where(last, me - 1, me + 1), tp),
            device_id_type=MESH,
        )
        halo.append(copy)

        @pl.when(jnp.logical_not(last))
        def _():
            copy.start()

    @pl.when(first)
    def _():
        window[:TOK, :] = jnp.zeros((TOK, channels), BF16)

    def tell(word, to, to_tp):
        pl.semaphore_signal(
            relay.at[word], inc=1, device_id=(to, to_tp), device_id_type=MESH
        )

    def blocks_at(step):
        return ((block + step < blocks, step), (block >= step, -step))

    def tell_blocks(word, step):
        for exists, d in blocks_at(step):
            @pl.when(exists)
            def _():
                tell(word, me + d * BLOCK, tp)

    def hear_blocks(word, step):
        up, down = blocks_at(step)
        pl.semaphore_wait(relay.at[word], jnp.where(up[0], 1, 0) + jnp.where(down[0], 1, 0))

    tell(TWO_TP, me, (tp + 1) % tp_size)

    @pl.when(is_owner)
    def _():
        for to in beside:
            tell(ROUND_1, to, tp)
        for exists, to in above:
            @pl.when(exists)
            def _():
                tell(ROUND_1, to, tp)

    in_copies = {}
    for i, (name, src, dst) in enumerate((
        ("taps", taps_h, taps), ("rate", rate_h, rate), ("residue", residue_h, residue),
        ("resid", resid_h, resid), ("q_mr", q_mr_h, q_mr), ("k_lr", k_lr_h, k_lr),
        ("gain", gain_h, gain_in), ("q_lr", q_lr_h, q_lr),
    )):
        in_copies[name] = pltpu.make_async_copy(src, dst, in_sem.at[i])
        in_copies[name].start()

    row_of = lax.broadcasted_iota(jnp.int32, (TOK, TOK), 0)
    col_of = lax.broadcasted_iota(jnp.int32, (TOK, TOK), 1)
    diagonal = row_of == col_of
    causal = col_of <= row_of
    for name in ("taps", "rate", "residue"):
        in_copies[name].wait()
    flip = ((row_of + col_of) % TOK == 0).astype(BF16)
    taps_rev[...] = jnp.dot(taps[...], flip, preferred_element_type=F32)
    weight_eff[...] = shared_steps(rate[...], residue[...])

    def mr_tables(j, carry):
        for i in range(PER_TILE):
            g = j * PER_TILE + i
            line = jnp.broadcast_to(taps_rev[pl.ds(g, 1), :], (TOK, TOK))
            square = pltpu.roll(line, 0, 1, stride=1, stride_axis=0)
            rows = pl.ds(pl.multiple_of(g * TOK, TOK), TOK)
            mr_tab[rows, :TOK] = jnp.where(causal, 0.0, square).astype(BF16)
            mr_tab[rows, TOK:] = jnp.where(causal, square, 0.0).astype(BF16)
        return carry

    lax.fori_loop(0, tiles, mr_tables, 0, unroll=4)

    row_group = row_of // POLES
    rates = jnp.concatenate([rate[...]] * PER_TILE, axis=0)
    weights = jnp.concatenate([weight_eff[...]] * PER_TILE, axis=0)
    backward = (TOK - 1 - col_of).astype(F32)
    forward = (col_of + 1).astype(F32)

    def of_rows(j, values):
        here = col_of == row_group + j * PER_TILE
        return jnp.sum(jnp.where(here, values, 0.0), axis=1, keepdims=True)

    def leave_table(j, carry):
        leave = jnp.exp(-of_rows(j, rates) * backward)
        rows = pl.ds(pl.multiple_of(j * TOK, TOK), TOK)
        high = leave.astype(BF16)
        leave_tab[rows, :TOK] = high
        leave_tab[rows, TOK : 2 * TOK] = (leave - high.astype(F32)).astype(BF16)
        leave_tab[rows, 2 * TOK :] = high
        weighted = of_rows(j, weights) * leave
        lines = [
            jnp.sum(weighted[i * POLES : (i + 1) * POLES], axis=0, keepdims=True)
            for i in range(PER_TILE)
        ]
        rows = pl.ds(pl.multiple_of(j * PER_TILE, PER_TILE), PER_TILE)
        impulse[rows, :] = pltpu.roll(jnp.concatenate(lines, axis=0), 1, 1)
        return carry

    def lr_tables(j, carry):
        for i in range(PER_TILE):
            g = j * PER_TILE + i
            line = jnp.broadcast_to(impulse[pl.ds(g, 1), :], (TOK, TOK))
            square = pltpu.roll(line, 0, 1, stride=1, stride_axis=0)
            rows = pl.ds(pl.multiple_of(g * TOK, TOK), TOK)
            square = jnp.where(causal, square, 0.0)
            high = square.astype(BF16)
            lr_tab[rows, :TOK] = high
            lr_tab[rows, TOK : 2 * TOK] = (square - high.astype(F32)).astype(BF16)
            lr_tab[rows, 2 * TOK :] = high
        return carry

    def entry_table(j, carry):
        entry = (of_rows(j, weights) * jnp.exp(-of_rows(j, rates) * forward)).T
        high = entry.astype(BF16)
        rows = pl.ds(pl.multiple_of(j * TOK, TOK), TOK)
        entry_tab[rows, :LANES] = high
        entry_tab[rows, LANES:] = (entry - high.astype(F32)).astype(BF16)
        return carry

    def own_lanes(stacked, rows):
        mask = lax.broadcasted_iota(jnp.int32, (rows, LANES), 1) // GROUP
        out = stacked[:rows]
        for i in range(1, PER_TILE):
            out = jnp.where(mask == i, stacked[i * rows : (i + 1) * rows], out)
        return out


    squares_sum = jnp.zeros((TOK, LANES), F32)
    for name in ("resid", "q_mr"):
        in_copies[name].wait()
    for c in range(len(CHUNKS)):
        @pl.when(jnp.logical_not(first))
        def _():
            halo[c].wait_recv()

        def mr_tile(j, acc):
            cols = pl.ds(pl.multiple_of(j * LANES, LANES), LANES)
            rows = pl.ds(pl.multiple_of(j * PER_TILE * TOK, TOK), PER_TILE * TOK)
            stacked = jnp.dot(mr_tab[rows, :], window[:, cols], preferred_element_type=F32)
            conv = own_lanes(stacked, TOK)
            result = (resid[:, cols].astype(F32) + q_mr[:, cols].astype(F32) * conv).astype(BF16)
            mixed[:, cols] = result
            result = result.astype(F32)
            return acc + result * result

        if c == 1:
            @pl.when(is_owner)
            def _():
                pl.semaphore_wait(relay.at[ROUND_1], 2 + n_above)
                for to in beside + [partner]:
                    tell(ROUND_2, to, tp)
                tell_blocks(BLOCKS_1, 1)

        if c == 3:
            @pl.when(is_owner)
            def _():
                pl.semaphore_wait(relay.at[ROUND_2], 3)
                for to in beside + [partner]:
                    tell(ROUND_3, to, tp)
                tell(ALL_OWNERS, me - 1, tp)

        squares_sum = lax.fori_loop(starts[c], starts[c] + CHUNKS[c], mr_tile, squares_sum, unroll=True)

    row_sum = jnp.sum(squares_sum, axis=1, keepdims=True)
    line = jnp.sum(jnp.where(diagonal, row_sum, 0.0), axis=0, keepdims=True)
    squares[tp] = jnp.broadcast_to(line, (8, TOK))
    pl.semaphore_wait(relay.at[TWO_TP], 1)
    tp_copies = []
    for d in (2, 1, 3):
        copy = pltpu.make_async_remote_copy(
            src_ref=squares.at[tp],
            dst_ref=squares.at[tp],
            send_sem=tp_send.at[d],
            recv_sem=tp_recv.at[d],
            device_id=(me, (tp + d) % tp_size),
            device_id_type=MESH,
        )
        copy.start()
        tp_copies.append(copy)
    mixed_copy = pltpu.make_async_copy(mixed, mixed_h, out_sem.at[0])
    mixed_copy.start()
    for name in ("k_lr", "gain", "q_lr"):
        in_copies[name].wait()

    gain[...] = gain_in[...].astype(F32)

    def gate_tile(j, carry):
        cols = pl.ds(pl.multiple_of(j * LANES, LANES), LANES)
        scaled = mixed[:, cols].astype(F32) * gain[pl.ds(j, 1), :]
        gated[:, cols] = scaled * k_lr[:, cols].astype(F32)
        return carry

    lax.fori_loop(0, tiles, leave_table, 0, unroll=4)
    lax.fori_loop(0, tiles, gate_tile, 0, unroll=4)

    @pl.when(is_owner)
    def _():
        hear_blocks(BLOCKS_1, 1)
        tell_blocks(BLOCKS_2, 2)

    for copy in tp_copies:
        copy.wait_recv()
    line = squares[0, :1, :]
    for d in range(1, tp_size):
        line = line + squares[d, :1, :]
    line = lax.rsqrt(line / (channels * tp_size) + 1e-06)
    scale = jnp.sum(jnp.where(diagonal, line, 0.0), axis=1, keepdims=True)

    lr_in = window

    for copy in halo:
        @pl.when(jnp.logical_not(last))
        def _():
            copy.wait_send()

    @pl.when(jnp.logical_not(is_owner))
    def _():
        pl.semaphore_wait(relay.at[ALL_OWNERS], 1)

    own_copies = []
    for s, (dz, dx) in enumerate(OWNER_STEPS):
        z_to, x_to = (z_at + dz) % 2, (x_at + dx) % 4
        owner = z_to * 4 + x_to
        for half in range(2):
            j = owner * 2 + half
            cols = pl.ds(pl.multiple_of(j * LANES, LANES), LANES)
            value = gated[:, cols] * scale
            high = value.astype(BF16)
            low = (value - high.astype(F32)).astype(BF16)
            lr_in[:TOK, cols] = high
            lr_in[TOK:, cols] = low
            rows = pl.ds(pl.multiple_of(j * LANES, LANES), LANES)
            stacked = jnp.dot(
                leave_tab[rows, :],
                jnp.concatenate([high, high, low], axis=0),
                preferred_element_type=F32,
            )
            states[s, half * POLES : (half + 1) * POLES, :] = own_lanes(stacked, POLES).astype(BF16)
        copy = pltpu.make_async_remote_copy(
            src_ref=states.at[s],
            dst_ref=gathered.at[member],
            send_sem=own_send.at[s],
            recv_sem=own_recv,
            device_id=(
                jnp.where(is_owner & ((dz, dx) == (0, 0)), me - 1, base + z_to * 8 + x_to * 2 + 1),
                tp,
            ),
            device_id_type=MESH,
        )
        own_copies.append(copy)
        if (dz, dx) == (0, 0):
            @pl.when(is_owner)
            def _():
                gathered[member] = states[s]

            @pl.when(jnp.logical_not(is_owner))
            def _():
                copy.start()
        else:
            copy.start()

    far = 4
    passes_far = is_owner & (block >= far) & (block < blocks - 1)

    @pl.when(passes_far)
    def _():
        hear_blocks(BLOCKS_2, 2)
        tell(BLOCKS_4, me - far * BLOCK, tp)

    def lr_conv_tile(j, carry):
        cols = pl.ds(pl.multiple_of(j * LANES, LANES), LANES)
        rows = pl.ds(pl.multiple_of(j * PER_TILE * TOK, TOK), PER_TILE * TOK)
        high, low = lr_in[:TOK, cols], lr_in[TOK:, cols]
        stacked = jnp.dot(
            lr_tab[rows, :], jnp.concatenate([high, high, low], axis=0), preferred_element_type=F32
        )
        local[:, cols] = own_lanes(stacked, TOK)
        return carry

    lax.fori_loop(0, tiles, lr_tables, 0, unroll=4)

    @pl.when(is_owner)
    def _():
        pl.semaphore_wait(relay.at[ROUND_3], 3)

    my_owner = z_at * 4 + x_at

    def total_copy(d, to):
        return pltpu.make_async_remote_copy(
            src_ref=total,
            dst_ref=totals.at[block],
            send_sem=tot_send.at[d],
            recv_sem=tot_recv.at[block],
            device_id=(to * BLOCK + member, tp),
            device_id_type=MESH,
        )

    back_steps = [(dz, dx, c) for dz, dx in OWNER_STEPS for c in (0, 1)]
    back_steps.remove((0, 0, 1))

    @pl.when(is_owner)
    def _():
        lane = lax.broadcasted_iota(jnp.int32, (LANES, 2 * LANES), 1)
        row = lax.broadcasted_iota(jnp.int32, (LANES, 2 * LANES), 0)
        spread = (row == my_owner * 2 * PER_TILE + lane // GROUP).astype(F32)
        wide_rate = jnp.dot(
            rate[...], spread, precision=lax.Precision.HIGHEST, preferred_element_type=F32
        )
        wide_rate = jnp.concatenate([wide_rate[:, :LANES], wide_rate[:, LANES:]], axis=0)
        through = jnp.exp(-wide_rate * TOK)
        through_block = jnp.exp(-wide_rate * (TOK * BLOCK))
        pltpu.make_async_copy(
            gathered.at[pl.ds(0, BLOCK - 1)], gathered.at[pl.ds(0, BLOCK - 1)], own_recv
        ).wait()
        state = jnp.zeros((2 * POLES, LANES), F32)
        for i in range(BLOCK):
            state = state * through + gathered[i].astype(F32)
        total[...] = state.astype(BF16)

        @pl.when(block < far)
        def _():
            hear_blocks(BLOCKS_2, 2)

        for d in NEAR_BLOCKS:
            @pl.when(block + d < blocks)
            def _():
                total_copy(d, block + d).start()

        lax.fori_loop(0, tiles // 2, lr_conv_tile, 0, unroll=4)

        def totals_to_far():
            pl.semaphore_wait(relay.at[BLOCKS_4], 1)
            for d in FAR_BLOCKS:
                @pl.when(block + d < blocks)
                def _():
                    total_copy(d, block + d).start()

        pl.when((block + far + 1 < blocks) & (block >= 2))(totals_to_far)
        lax.fori_loop(tiles // 2, tiles, lr_conv_tile, 0, unroll=4)

        carried = jnp.zeros((2 * POLES, LANES), F32)
        for b in range(blocks - 1):
            @pl.when(b < block)
            def _():
                pltpu.make_async_copy(totals.at[b], totals.at[b], tot_recv.at[b]).wait()

        for b in range(blocks - 1):
            carried = jnp.where(b < block, carried * through_block + totals[b].astype(F32), carried)
        for i in range(BLOCK):
            carry_out[i] = carried.astype(BF16)
            if i < BLOCK - 1:
                carried = carried * through + gathered[i].astype(F32)
        for s, (dz, dx, c) in enumerate(back_steps):
            to = ((z_at + dz) % 2) * 8 + ((x_at + dx) % 4) * 2 + c
            pltpu.make_async_remote_copy(
                src_ref=carry_out.at[to],
                dst_ref=carry_in.at[my_owner],
                send_sem=back_send.at[s],
                recv_sem=back_recv.at[my_owner],
                device_id=(base + to, tp),
                device_id_type=MESH,
            ).start()
        carry_in[my_owner] = carry_out[member]
        lax.fori_loop(0, tiles, entry_table, 0, unroll=4)
        pl.when(block < 2)(totals_to_far)

    @pl.when(jnp.logical_not(is_owner))
    def _():
        lax.fori_loop(0, tiles, lr_conv_tile, 0, unroll=4)
        lax.fori_loop(0, tiles, entry_table, 0, unroll=4)

    lane_group = lax.broadcasted_iota(jnp.int32, (POLES, LANES), 1) // GROUP
    pole_masks = [(lane_group == i).astype(F32).astype(BF16) for i in range(PER_TILE)]

    def out_tile(owner, half):
        cols = pl.ds(pl.multiple_of((owner * 2 + half) * LANES, LANES), LANES)
        rows = pl.ds(pl.multiple_of((owner * 2 + half) * TOK, TOK), TOK)
        came = carry_in[owner, half * POLES : (half + 1) * POLES, :]
        spread = [came * mask for mask in pole_masks]
        spread = jnp.concatenate(spread + spread, axis=0)
        incoming = jnp.dot(entry_tab[rows, :], spread, preferred_element_type=F32)
        conv = local[:, cols] + incoming
        lr_out[:, cols] = (q_lr[:, cols].astype(F32) * conv).astype(BF16)

    out_copies = []
    for s, (dz, dx) in enumerate(reversed(OWNER_STEPS)):
        owner = ((z_at + dz) % 2) * 4 + (x_at + dx) % 4

        def arrive():
            pltpu.make_async_copy(carry_in.at[owner], carry_in.at[owner], back_recv.at[owner]).wait()

        if (dz, dx) == (0, 0):
            pl.when(jnp.logical_not(is_owner))(arrive)
        else:
            arrive()
        for half in range(2):
            out_tile(owner, half)
        cols = pl.ds(pl.multiple_of(owner * 2 * LANES, 2 * LANES), 2 * LANES)
        copy = pltpu.make_async_copy(lr_out.at[:, cols], out_h.at[:, cols], out_sem.at[1 + s])
        copy.start()
        out_copies.append(copy)

    for copy in tp_copies:
        copy.wait_send()
    for (dz, dx), copy in zip(OWNER_STEPS, own_copies):
        if (dz, dx) == (0, 0):
            @pl.when(jnp.logical_not(is_owner))
            def _():
                copy.wait_send()
        else:
            copy.wait_send()

    @pl.when(is_owner)
    def _():
        @pl.when(block == blocks - 1)
        def _():
            hear_blocks(BLOCKS_2, 2)

        for d in NEAR_BLOCKS + FAR_BLOCKS:
            @pl.when(block + d < blocks)
            def _():
                total_copy(d, block + d).wait_send()
        for s in range(len(back_steps)):
            pltpu.make_async_copy(carry_out.at[0], carry_out.at[0], back_send.at[s]).wait()

    mixed_copy.wait()
    for copy in out_copies:
        copy.wait()


def hand_over(mixed, lr_out, mixed_to, lr_out_to, held, in_sems, out_sems):
    rows = TOK // HAND_PIECES
    inward, outward = [], []
    for c in range(HAND_PIECES):
        part = pl.ds(c * rows, rows)
        for i, (src, dst) in enumerate(((mixed, mixed_to), (lr_out, lr_out_to))):
            inward.append(pltpu.make_async_copy(src.at[part], held.at[i, part], in_sems.at[i, c]))
            outward.append(pltpu.make_async_copy(held.at[i, part], dst.at[part], out_sems.at[i, c]))
    for copy in inward:
        copy.start()
    for came, copy in zip(inward, outward):
        came.wait()
        copy.start()
    for copy in outward:
        copy.wait()


def per_device(resid, q_mr, k_mr, v_mr, mr_taps, norm_gain, q_lr, k_lr, pole_rate, residue):
    tok, channels = resid.shape
    tp_size = lax.axis_size("tp")
    blocks = lax.axis_size("ctx") // BLOCK
    tiles = channels // LANES
    groups = channels // GROUP
    big = pltpu.VMEM((tok, channels), BF16)
    scratch = [
        big, big, big, big, big, big,
        pltpu.VMEM((groups, TOK), BF16),
        pltpu.VMEM((tiles, LANES), F32),
        pltpu.VMEM((tiles, LANES), BF16),
        pltpu.VMEM((POLES, groups), F32),
        pltpu.VMEM((POLES, groups), F32),
        pltpu.VMEM((2 * TOK, channels), BF16),
        pltpu.VMEM((groups * TOK, 2 * TOK), BF16),
        pltpu.VMEM((groups * TOK, 3 * TOK), BF16),
        pltpu.VMEM((groups * POLES, 3 * TOK), BF16),
        pltpu.VMEM((tiles * TOK, 2 * LANES), BF16),
        pltpu.VMEM((groups, TOK), F32),
        pltpu.VMEM((POLES, groups), F32),
        pltpu.VMEM((groups, TOK), F32),
        big,
        pltpu.VMEM((tok, channels), F32),
        pltpu.VMEM((tok, channels), F32),
        big,
        pltpu.VMEM((tp_size, 8, TOK), F32),
        pltpu.VMEM((OWNERS, 2 * POLES, LANES), BF16),
        pltpu.VMEM((BLOCK, 2 * POLES, LANES), BF16),
        pltpu.VMEM((2 * POLES, LANES), BF16),
        pltpu.VMEM((blocks, 2 * POLES, LANES), BF16),
        pltpu.VMEM((BLOCK, 2 * POLES, LANES), BF16),
        pltpu.VMEM((OWNERS, 2 * POLES, LANES), BF16),
        pltpu.SemaphoreType.DMA((2, len(CHUNKS))),
        pltpu.SemaphoreType.DMA((8,)),
        pltpu.SemaphoreType.DMA((1 + OWNERS,)),
        pltpu.SemaphoreType.DMA((len(CHUNKS),)),
        pltpu.SemaphoreType.DMA((len(CHUNKS),)),
        pltpu.SemaphoreType.DMA((tp_size,)),
        pltpu.SemaphoreType.DMA((tp_size,)),
        pltpu.SemaphoreType.DMA((OWNERS,)),
        pltpu.SemaphoreType.DMA,
        pltpu.SemaphoreType.DMA((blocks,)),
        pltpu.SemaphoreType.DMA((blocks,)),
        pltpu.SemaphoreType.DMA((2 * OWNERS,)),
        pltpu.SemaphoreType.DMA((OWNERS,)),
        pltpu.SemaphoreType.REGULAR((8,)),
    ]
    in_place = pl.BlockSpec(memory_space=pl.ANY)
    out = jax.ShapeDtypeStruct((tok, channels), BF16)
    results = pl.pallas_call(
        functools.partial(kernel, blocks, tp_size),
        out_shape=(out, out),
        in_specs=[in_place] * 10,
        out_specs=(in_place, in_place),
        scratch_shapes=scratch,
        compiler_params=pltpu.CompilerParams(
            collective_id=0, has_side_effects=True, vmem_limit_bytes=56 * 1024 * 1024
        ),
        name="mixers",
    )(resid, q_mr, k_mr, v_mr, mr_taps, norm_gain.reshape(tiles, LANES), q_lr, k_lr, pole_rate, residue)
    return pl.pallas_call(
        hand_over,
        out_shape=(out, out),
        in_specs=[in_place] * 2,
        out_specs=(in_place, in_place),
        scratch_shapes=[
            pltpu.VMEM((2, tok, channels), BF16),
            pltpu.SemaphoreType.DMA((2, HAND_PIECES)),
            pltpu.SemaphoreType.DMA((2, HAND_PIECES)),
        ],
        compiler_params=pltpu.CompilerParams(vmem_limit_bytes=56 * 1024 * 1024),
        name="hand_over",
    )(*results)


def solution(mesh):
    placed = (
        P("ctx", "tp"),
        P("ctx", "tp"),
        P("ctx", "tp"),
        P("ctx", "tp"),
        P("tp", None),
        P("tp"),
        P("ctx", "tp"),
        P("ctx", "tp"),
        P(None, "tp"),
        P(None, "tp"),
    )
    return jax.shard_map(
        per_device,
        mesh=mesh,
        in_specs=placed,
        out_specs=(P("ctx", "tp"), P("ctx", "tp")),
        check_vma=False,
    )
```

```python
import functools

import jax
import jax.numpy as jnp
from jax import lax
from jax.experimental import pallas as pl
from jax.experimental.pallas import tpu as pltpu
from jax.sharding import PartitionSpec as P

F32 = jnp.float32
BF16 = jnp.bfloat16
MESH = pl.DeviceIdType.MESH

TOK = 128
LANES = 128
GROUP = 16
PER_TILE = LANES // GROUP
POLES = 16
BLOCK = 16
OWNERS = 8
CHUNKS = (4, 4, 4, 3, 1)

TWO_TP, ROUND_1, ROUND_2, ROUND_3, ALL_OWNERS, BLOCKS_1, BLOCKS_2, BLOCKS_4 = range(8)

HAND_PIECES = 4

OWNER_STEPS = ((1, 2), (0, 2), (1, 1), (1, 3), (0, 1), (0, 3), (1, 0), (0, 0))
NEAR_BLOCKS = (4, 3, 2, 1)
FAR_BLOCKS = (5, 6, 7)


def shared_steps(rate, residue):
    y = 2.0 * rate
    series = jnp.ones_like(y)
    for order in range(10, 1, -1):
        series = 1.0 - series * y / order
    gap = jnp.where(y < 0.5, y * series, 1.0 - jnp.exp(-y))
    return residue * jnp.sqrt(gap)


def kernel(
    blocks,
    tp_size,
    resid_h, q_mr_h, k_mr_h, v_mr_h, taps_h, gain_h, q_lr_h, k_lr_h, rate_h, residue_h,
    mixed_h, out_h,
    k_mr, v_mr, resid, q_mr, k_lr, q_lr, taps, gain, gain_in, rate, residue,
    window, mr_tab, lr_tab, leave_tab, entry_tab, taps_rev, weight_eff, impulse,
    mixed, gated, local, lr_out, squares, states, gathered, total, totals, carry_out, carry_in,
    kv_sem, in_sem, out_sem, halo_send, halo_recv, tp_send, tp_recv,
    own_send, own_recv, tot_send, tot_recv, back_send, back_recv, relay,
):
    me = lax.axis_index("ctx")
    tp = lax.axis_index("tp")
    shards = blocks * BLOCK
    channels = k_mr.shape[1]
    tiles = channels // LANES
    starts = [sum(CHUNKS[:c]) for c in range(len(CHUNKS))]
    block = me // BLOCK
    member = me % BLOCK
    base = block * BLOCK
    core = me % 2
    x_at = (me // 2) % 4
    z_at = (me // 8) % 2
    first = me == 0
    last = me == shards - 1
    is_owner = core == 1

    totals[...] = jnp.zeros_like(totals)

    barrier = pltpu.get_barrier_semaphore()

    def greet(ctx, tp_to):
        pl.semaphore_signal(barrier, inc=1, device_id=(ctx, tp_to), device_id_type=MESH)

    @pl.when(jnp.logical_not(last))
    def _():
        greet(me + 1, tp)

    @pl.when(jnp.logical_not(first))
    def _():
        greet(me - 1, tp)

    for d in (1, tp_size - 1):
        greet(me, (tp + d) % tp_size)
    plane = me // 8
    planes = shards // 8
    beside = [plane * 8 + ((x_at + d) % 4) * 2 + core for d in (1, 3)]
    above = ((plane + 1 < planes, me + 8), (plane > 0, me - 8))
    n_above = jnp.where(plane + 1 < planes, 1, 0) + jnp.where(plane > 0, 1, 0)
    partner = base + (1 - z_at) * 8 + x_at * 2 + core

    @pl.when(is_owner)
    def _():
        for to in beside:
            greet(to, tp)
        for exists, to in above:
            @pl.when(exists)
            def _():
                greet(to, tp)

    kv_copies = []
    for c in range(len(CHUNKS)):
        cols = pl.ds(starts[c] * LANES, CHUNKS[c] * LANES)
        pair = []
        for i, (src, dst) in enumerate(((k_mr_h, k_mr), (v_mr_h, v_mr))):
            copy = pltpu.make_async_copy(src.at[:, cols], dst.at[:, cols], kv_sem.at[i, c])
            copy.start()
            pair.append(copy)
        kv_copies.append(pair)
    halo = []
    for c in range(len(CHUNKS)):
        for copy in kv_copies[c]:
            copy.wait()
        cols = pl.ds(starts[c] * LANES, CHUNKS[c] * LANES)
        window[TOK:, cols] = (k_mr[:, cols].astype(F32) * v_mr[:, cols].astype(F32)).astype(BF16)
        if c == 0:
            ends = jnp.where(first, 0, 1) + jnp.where(last, 0, 1)
            near = jnp.where(is_owner, 2 + 2 + n_above, 2)
            pl.semaphore_wait(barrier, ends + near)

        copy = pltpu.make_async_remote_copy(
            src_ref=window.at[pl.ds(TOK, TOK), cols],
            dst_ref=window.at[pl.ds(0, TOK), cols],
            send_sem=halo_send.at[c],
            recv_sem=halo_recv.at[c],
            device_id=(jnp.where(last, me - 1, me + 1), tp),
            device_id_type=MESH,
        )
        halo.append(copy)

        @pl.when(jnp.logical_not(last))
        def _():
            copy.start()

    @pl.when(first)
    def _():
        window[:TOK, :] = jnp.zeros((TOK, channels), BF16)

    def tell(word, to, to_tp):
        pl.semaphore_signal(
            relay.at[word], inc=1, device_id=(to, to_tp), device_id_type=MESH
        )

    def blocks_at(step):
        return ((block + step < blocks, step), (block >= step, -step))

    def tell_blocks(word, step):
        for exists, d in blocks_at(step):
            @pl.when(exists)
            def _():
                tell(word, me + d * BLOCK, tp)

    def hear_blocks(word, step):
        up, down = blocks_at(step)
        pl.semaphore_wait(relay.at[word], jnp.where(up[0], 1, 0) + jnp.where(down[0], 1, 0))

    tell(TWO_TP, me, (tp + 1) % tp_size)

    @pl.when(is_owner)
    def _():
        for to in beside:
            tell(ROUND_1, to, tp)
        for exists, to in above:
            @pl.when(exists)
            def _():
                tell(ROUND_1, to, tp)

    in_copies = {}
    for i, (name, src, dst) in enumerate((
        ("taps", taps_h, taps), ("rate", rate_h, rate), ("residue", residue_h, residue),
        ("resid", resid_h, resid), ("q_mr", q_mr_h, q_mr), ("k_lr", k_lr_h, k_lr),
        ("gain", gain_h, gain_in), ("q_lr", q_lr_h, q_lr),
    )):
        in_copies[name] = pltpu.make_async_copy(src, dst, in_sem.at[i])
        in_copies[name].start()

    row_of = lax.broadcasted_iota(jnp.int32, (TOK, TOK), 0)
    col_of = lax.broadcasted_iota(jnp.int32, (TOK, TOK), 1)
    diagonal = row_of == col_of
    causal = col_of <= row_of
    for name in ("taps", "rate", "residue"):
        in_copies[name].wait()
    flip = ((row_of + col_of) % TOK == 0).astype(BF16)
    taps_rev[...] = jnp.dot(taps[...], flip, preferred_element_type=F32)
    weight_eff[...] = shared_steps(rate[...], residue[...])

    def mr_tables(j, carry):
        for i in range(PER_TILE):
            g = j * PER_TILE + i
            line = jnp.broadcast_to(taps_rev[pl.ds(g, 1), :], (TOK, TOK))
            square = pltpu.roll(line, 0, 1, stride=1, stride_axis=0)
            rows = pl.ds(pl.multiple_of(g * TOK, TOK), TOK)
            mr_tab[rows, :TOK] = jnp.where(causal, 0.0, square).astype(BF16)
            mr_tab[rows, TOK:] = jnp.where(causal, square, 0.0).astype(BF16)
        return carry

    lax.fori_loop(0, tiles, mr_tables, 0, unroll=4)

    row_group = row_of // POLES
    rates = jnp.concatenate([rate[...]] * PER_TILE, axis=0)
    weights = jnp.concatenate([weight_eff[...]] * PER_TILE, axis=0)
    backward = (TOK - 1 - col_of).astype(F32)
    forward = (col_of + 1).astype(F32)

    def of_rows(j, values):
        here = col_of == row_group + j * PER_TILE
        return jnp.sum(jnp.where(here, values, 0.0), axis=1, keepdims=True)

    def leave_table(j, carry):
        leave = jnp.exp(-of_rows(j, rates) * backward)
        rows = pl.ds(pl.multiple_of(j * TOK, TOK), TOK)
        high = leave.astype(BF16)
        leave_tab[rows, :TOK] = high
        leave_tab[rows, TOK : 2 * TOK] = (leave - high.astype(F32)).astype(BF16)
        leave_tab[rows, 2 * TOK :] = high
        weighted = of_rows(j, weights) * leave
        lines = [
            jnp.sum(weighted[i * POLES : (i + 1) * POLES], axis=0, keepdims=True)
            for i in range(PER_TILE)
        ]
        rows = pl.ds(pl.multiple_of(j * PER_TILE, PER_TILE), PER_TILE)
        impulse[rows, :] = pltpu.roll(jnp.concatenate(lines, axis=0), 1, 1)
        return carry

    def lr_tables(j, carry):
        for i in range(PER_TILE):
            g = j * PER_TILE + i
            line = jnp.broadcast_to(impulse[pl.ds(g, 1), :], (TOK, TOK))
            square = pltpu.roll(line, 0, 1, stride=1, stride_axis=0)
            rows = pl.ds(pl.multiple_of(g * TOK, TOK), TOK)
            square = jnp.where(causal, square, 0.0)
            high = square.astype(BF16)
            lr_tab[rows, :TOK] = high
            lr_tab[rows, TOK : 2 * TOK] = (square - high.astype(F32)).astype(BF16)
            lr_tab[rows, 2 * TOK :] = high
        return carry

    def entry_table(j, carry):
        entry = (of_rows(j, weights) * jnp.exp(-of_rows(j, rates) * forward)).T
        high = entry.astype(BF16)
        rows = pl.ds(pl.multiple_of(j * TOK, TOK), TOK)
        entry_tab[rows, :LANES] = high
        entry_tab[rows, LANES:] = (entry - high.astype(F32)).astype(BF16)
        return carry

    def own_lanes(stacked, rows):
        mask = lax.broadcasted_iota(jnp.int32, (rows, LANES), 1) // GROUP
        out = stacked[:rows]
        for i in range(1, PER_TILE):
            out = jnp.where(mask == i, stacked[i * rows : (i + 1) * rows], out)
        return out


    squares_sum = jnp.zeros((TOK, LANES), F32)
    for name in ("resid", "q_mr"):
        in_copies[name].wait()
    for c in range(len(CHUNKS)):
        @pl.when(jnp.logical_not(first))
        def _():
            halo[c].wait_recv()

        def mr_tile(j, acc):
            cols = pl.ds(pl.multiple_of(j * LANES, LANES), LANES)
            rows = pl.ds(pl.multiple_of(j * PER_TILE * TOK, TOK), PER_TILE * TOK)
            stacked = jnp.dot(mr_tab[rows, :], window[:, cols], preferred_element_type=F32)
            conv = own_lanes(stacked, TOK)
            result = (resid[:, cols].astype(F32) + q_mr[:, cols].astype(F32) * conv).astype(BF16)
            mixed[:, cols] = result
            result = result.astype(F32)
            return acc + result * result

        if c == 1:
            @pl.when(is_owner)
            def _():
                pl.semaphore_wait(relay.at[ROUND_1], 2 + n_above)
                for to in beside + [partner]:
                    tell(ROUND_2, to, tp)
                tell_blocks(BLOCKS_1, 1)

        if c == 3:
            @pl.when(is_owner)
            def _():
                pl.semaphore_wait(relay.at[ROUND_2], 3)
                for to in beside + [partner]:
                    tell(ROUND_3, to, tp)
                tell(ALL_OWNERS, me - 1, tp)

        squares_sum = lax.fori_loop(starts[c], starts[c] + CHUNKS[c], mr_tile, squares_sum, unroll=True)

    row_sum = jnp.sum(squares_sum, axis=1, keepdims=True)
    line = jnp.sum(jnp.where(diagonal, row_sum, 0.0), axis=0, keepdims=True)
    squares[tp] = jnp.broadcast_to(line, (8, TOK))
    pl.semaphore_wait(relay.at[TWO_TP], 1)
    tp_copies = []
    for d in (2, 1, 3):
        copy = pltpu.make_async_remote_copy(
            src_ref=squares.at[tp],
            dst_ref=squares.at[tp],
            send_sem=tp_send.at[d],
            recv_sem=tp_recv.at[d],
            device_id=(me, (tp + d) % tp_size),
            device_id_type=MESH,
        )
        copy.start()
        tp_copies.append(copy)
    @pl.when(is_owner)
    def _():
        hear_blocks(BLOCKS_1, 1)
        tell_blocks(BLOCKS_2, 2)

    mixed_copy = pltpu.make_async_copy(mixed, mixed_h, out_sem.at[0])
    mixed_copy.start()
    for name in ("k_lr", "gain", "q_lr"):
        in_copies[name].wait()

    gain[...] = gain_in[...].astype(F32)

    def gate_tile(j, carry):
        cols = pl.ds(pl.multiple_of(j * LANES, LANES), LANES)
        scaled = mixed[:, cols].astype(F32) * gain[pl.ds(j, 1), :]
        gated[:, cols] = scaled * k_lr[:, cols].astype(F32)
        return carry

    lax.fori_loop(0, tiles, leave_table, 0, unroll=4)
    lax.fori_loop(0, tiles, gate_tile, 0, unroll=4)

    for copy in tp_copies:
        copy.wait_recv()
    line = squares[0, :1, :]
    for d in range(1, tp_size):
        line = line + squares[d, :1, :]
    line = lax.rsqrt(line / (channels * tp_size) + 1e-06)
    scale = jnp.sum(jnp.where(diagonal, line, 0.0), axis=1, keepdims=True)

    lr_in = window

    for copy in halo:
        @pl.when(jnp.logical_not(last))
        def _():
            copy.wait_send()

    @pl.when(jnp.logical_not(is_owner))
    def _():
        pl.semaphore_wait(relay.at[ALL_OWNERS], 1)

    own_copies = []
    for s, (dz, dx) in enumerate(OWNER_STEPS):
        z_to, x_to = (z_at + dz) % 2, (x_at + dx) % 4
        owner = z_to * 4 + x_to
        for half in range(2):
            j = owner * 2 + half
            cols = pl.ds(pl.multiple_of(j * LANES, LANES), LANES)
            value = gated[:, cols] * scale
            high = value.astype(BF16)
            low = (value - high.astype(F32)).astype(BF16)
            lr_in[:TOK, cols] = high
            lr_in[TOK:, cols] = low
            rows = pl.ds(pl.multiple_of(j * LANES, LANES), LANES)
            stacked = jnp.dot(
                leave_tab[rows, :],
                jnp.concatenate([high, high, low], axis=0),
                preferred_element_type=F32,
            )
            states[s, half * POLES : (half + 1) * POLES, :] = own_lanes(stacked, POLES).astype(BF16)
        copy = pltpu.make_async_remote_copy(
            src_ref=states.at[s],
            dst_ref=gathered.at[member],
            send_sem=own_send.at[s],
            recv_sem=own_recv,
            device_id=(
                jnp.where(is_owner & ((dz, dx) == (0, 0)), me - 1, base + z_to * 8 + x_to * 2 + 1),
                tp,
            ),
            device_id_type=MESH,
        )
        own_copies.append(copy)
        if (dz, dx) == (0, 0):
            @pl.when(is_owner)
            def _():
                gathered[member] = states[s]

            @pl.when(jnp.logical_not(is_owner))
            def _():
                copy.start()
        else:
            copy.start()

    far = 4
    passes_far = is_owner & (block >= far) & (block < blocks - 1)

    @pl.when(passes_far)
    def _():
        hear_blocks(BLOCKS_2, 2)
        tell(BLOCKS_4, me - far * BLOCK, tp)

    def lr_conv_tile(j, carry):
        cols = pl.ds(pl.multiple_of(j * LANES, LANES), LANES)
        rows = pl.ds(pl.multiple_of(j * PER_TILE * TOK, TOK), PER_TILE * TOK)
        high, low = lr_in[:TOK, cols], lr_in[TOK:, cols]
        stacked = jnp.dot(
            lr_tab[rows, :], jnp.concatenate([high, high, low], axis=0), preferred_element_type=F32
        )
        local[:, cols] = own_lanes(stacked, TOK)
        return carry

    lax.fori_loop(0, tiles, lr_tables, 0, unroll=4)

    @pl.when(is_owner)
    def _():
        pl.semaphore_wait(relay.at[ROUND_3], 3)

    my_owner = z_at * 4 + x_at

    def total_copy(d, to):
        return pltpu.make_async_remote_copy(
            src_ref=total,
            dst_ref=totals.at[block],
            send_sem=tot_send.at[d],
            recv_sem=tot_recv.at[block],
            device_id=(to * BLOCK + member, tp),
            device_id_type=MESH,
        )

    back_steps = [(dz, dx, c) for dz, dx in OWNER_STEPS for c in (0, 1)]
    back_steps.remove((0, 0, 1))

    @pl.when(is_owner)
    def _():
        lane = lax.broadcasted_iota(jnp.int32, (LANES, 2 * LANES), 1)
        row = lax.broadcasted_iota(jnp.int32, (LANES, 2 * LANES), 0)
        spread = (row == my_owner * 2 * PER_TILE + lane // GROUP).astype(F32)
        wide_rate = jnp.dot(
            rate[...], spread, precision=lax.Precision.HIGHEST, preferred_element_type=F32
        )
        wide_rate = jnp.concatenate([wide_rate[:, :LANES], wide_rate[:, LANES:]], axis=0)
        through = jnp.exp(-wide_rate * TOK)
        through_block = jnp.exp(-wide_rate * (TOK * BLOCK))
        pltpu.make_async_copy(
            gathered.at[pl.ds(0, BLOCK - 1)], gathered.at[pl.ds(0, BLOCK - 1)], own_recv
        ).wait()
        state = jnp.zeros((2 * POLES, LANES), F32)
        for i in range(BLOCK):
            state = state * through + gathered[i].astype(F32)
        total[...] = state.astype(BF16)

        @pl.when(block < far)
        def _():
            hear_blocks(BLOCKS_2, 2)

        for d in NEAR_BLOCKS:
            @pl.when(block + d < blocks)
            def _():
                total_copy(d, block + d).start()

        lax.fori_loop(0, tiles // 4, lr_conv_tile, 0, unroll=4)

        def totals_to_far():
            pl.semaphore_wait(relay.at[BLOCKS_4], 1)
            for d in FAR_BLOCKS:
                @pl.when(block + d < blocks)
                def _():
                    total_copy(d, block + d).start()

        pl.when((block + far + 1 < blocks) & (block >= 2))(totals_to_far)
        lax.fori_loop(tiles // 4, tiles, lr_conv_tile, 0, unroll=4)

        carried = jnp.zeros((2 * POLES, LANES), F32)
        for b in range(blocks - 1):
            @pl.when(b < block)
            def _():
                pltpu.make_async_copy(totals.at[b], totals.at[b], tot_recv.at[b]).wait()

        for b in range(blocks - 1):
            carried = jnp.where(b < block, carried * through_block + totals[b].astype(F32), carried)
        for i in range(BLOCK):
            carry_out[i] = carried.astype(BF16)
            if i < BLOCK - 1:
                carried = carried * through + gathered[i].astype(F32)
        for s, (dz, dx, c) in enumerate(back_steps):
            to = ((z_at + dz) % 2) * 8 + ((x_at + dx) % 4) * 2 + c
            pltpu.make_async_remote_copy(
                src_ref=carry_out.at[to],
                dst_ref=carry_in.at[my_owner],
                send_sem=back_send.at[s],
                recv_sem=back_recv.at[my_owner],
                device_id=(base + to, tp),
                device_id_type=MESH,
            ).start()
        carry_in[my_owner] = carry_out[member]
        pl.when(block == 1)(totals_to_far)
        lax.fori_loop(0, tiles, entry_table, 0, unroll=4)
        pl.when(block == 0)(totals_to_far)

    @pl.when(jnp.logical_not(is_owner))
    def _():
        lax.fori_loop(0, tiles, lr_conv_tile, 0, unroll=4)
        lax.fori_loop(0, tiles, entry_table, 0, unroll=4)

    lane_group = lax.broadcasted_iota(jnp.int32, (POLES, LANES), 1) // GROUP
    pole_masks = [(lane_group == i).astype(F32).astype(BF16) for i in range(PER_TILE)]

    def out_tile(owner, half):
        cols = pl.ds(pl.multiple_of((owner * 2 + half) * LANES, LANES), LANES)
        rows = pl.ds(pl.multiple_of((owner * 2 + half) * TOK, TOK), TOK)
        came = carry_in[owner, half * POLES : (half + 1) * POLES, :]
        spread = [came * mask for mask in pole_masks]
        spread = jnp.concatenate(spread + spread, axis=0)
        incoming = jnp.dot(entry_tab[rows, :], spread, preferred_element_type=F32)
        conv = local[:, cols] + incoming
        lr_out[:, cols] = (q_lr[:, cols].astype(F32) * conv).astype(BF16)

    out_copies = []
    for s, (dz, dx) in enumerate(reversed(OWNER_STEPS)):
        owner = ((z_at + dz) % 2) * 4 + (x_at + dx) % 4

        def arrive():
            pltpu.make_async_copy(carry_in.at[owner], carry_in.at[owner], back_recv.at[owner]).wait()

        if (dz, dx) == (0, 0):
            pl.when(jnp.logical_not(is_owner))(arrive)
        else:
            arrive()
        for half in range(2):
            out_tile(owner, half)
        cols = pl.ds(pl.multiple_of(owner * 2 * LANES, 2 * LANES), 2 * LANES)
        copy = pltpu.make_async_copy(lr_out.at[:, cols], out_h.at[:, cols], out_sem.at[1 + s])
        copy.start()
        out_copies.append(copy)

    for copy in tp_copies:
        copy.wait_send()
    for (dz, dx), copy in zip(OWNER_STEPS, own_copies):
        if (dz, dx) == (0, 0):
            @pl.when(jnp.logical_not(is_owner))
            def _():
                copy.wait_send()
        else:
            copy.wait_send()

    @pl.when(is_owner)
    def _():
        @pl.when(block == blocks - 1)
        def _():
            hear_blocks(BLOCKS_2, 2)

        for d in NEAR_BLOCKS + FAR_BLOCKS:
            @pl.when(block + d < blocks)
            def _():
                total_copy(d, block + d).wait_send()
        for s in range(len(back_steps)):
            pltpu.make_async_copy(carry_out.at[0], carry_out.at[0], back_send.at[s]).wait()

    mixed_copy.wait()
    for copy in out_copies:
        copy.wait()


def hand_over(mixed, lr_out, mixed_to, lr_out_to, held, in_sems, out_sems):
    rows = TOK // HAND_PIECES
    inward, outward = [], []
    for c in range(HAND_PIECES):
        part = pl.ds(c * rows, rows)
        for i, (src, dst) in enumerate(((mixed, mixed_to), (lr_out, lr_out_to))):
            inward.append(pltpu.make_async_copy(src.at[part], held.at[i, part], in_sems.at[i, c]))
            outward.append(pltpu.make_async_copy(held.at[i, part], dst.at[part], out_sems.at[i, c]))
    for copy in inward:
        copy.start()
    for came, copy in zip(inward, outward):
        came.wait()
        copy.start()
    for copy in outward:
        copy.wait()


def per_device(resid, q_mr, k_mr, v_mr, mr_taps, norm_gain, q_lr, k_lr, pole_rate, residue):
    tok, channels = resid.shape
    tp_size = lax.axis_size("tp")
    blocks = lax.axis_size("ctx") // BLOCK
    tiles = channels // LANES
    groups = channels // GROUP
    big = pltpu.VMEM((tok, channels), BF16)
    scratch = [
        big, big, big, big, big, big,
        pltpu.VMEM((groups, TOK), BF16),
        pltpu.VMEM((tiles, LANES), F32),
        pltpu.VMEM((tiles, LANES), BF16),
        pltpu.VMEM((POLES, groups), F32),
        pltpu.VMEM((POLES, groups), F32),
        pltpu.VMEM((2 * TOK, channels), BF16),
        pltpu.VMEM((groups * TOK, 2 * TOK), BF16),
        pltpu.VMEM((groups * TOK, 3 * TOK), BF16),
        pltpu.VMEM((groups * POLES, 3 * TOK), BF16),
        pltpu.VMEM((tiles * TOK, 2 * LANES), BF16),
        pltpu.VMEM((groups, TOK), F32),
        pltpu.VMEM((POLES, groups), F32),
        pltpu.VMEM((groups, TOK), F32),
        big,
        pltpu.VMEM((tok, channels), F32),
        pltpu.VMEM((tok, channels), F32),
        big,
        pltpu.VMEM((tp_size, 8, TOK), F32),
        pltpu.VMEM((OWNERS, 2 * POLES, LANES), BF16),
        pltpu.VMEM((BLOCK, 2 * POLES, LANES), BF16),
        pltpu.VMEM((2 * POLES, LANES), BF16),
        pltpu.VMEM((blocks, 2 * POLES, LANES), BF16),
        pltpu.VMEM((BLOCK, 2 * POLES, LANES), BF16),
        pltpu.VMEM((OWNERS, 2 * POLES, LANES), BF16),
        pltpu.SemaphoreType.DMA((2, len(CHUNKS))),
        pltpu.SemaphoreType.DMA((8,)),
        pltpu.SemaphoreType.DMA((1 + OWNERS,)),
        pltpu.SemaphoreType.DMA((len(CHUNKS),)),
        pltpu.SemaphoreType.DMA((len(CHUNKS),)),
        pltpu.SemaphoreType.DMA((tp_size,)),
        pltpu.SemaphoreType.DMA((tp_size,)),
        pltpu.SemaphoreType.DMA((OWNERS,)),
        pltpu.SemaphoreType.DMA,
        pltpu.SemaphoreType.DMA((blocks,)),
        pltpu.SemaphoreType.DMA((blocks,)),
        pltpu.SemaphoreType.DMA((2 * OWNERS,)),
        pltpu.SemaphoreType.DMA((OWNERS,)),
        pltpu.SemaphoreType.REGULAR((8,)),
    ]
    in_place = pl.BlockSpec(memory_space=pl.ANY)
    out = jax.ShapeDtypeStruct((tok, channels), BF16)
    results = pl.pallas_call(
        functools.partial(kernel, blocks, tp_size),
        out_shape=(out, out),
        in_specs=[in_place] * 10,
        out_specs=(in_place, in_place),
        scratch_shapes=scratch,
        compiler_params=pltpu.CompilerParams(
            collective_id=0, has_side_effects=True, vmem_limit_bytes=56 * 1024 * 1024
        ),
        name="mixers",
    )(resid, q_mr, k_mr, v_mr, mr_taps, norm_gain.reshape(tiles, LANES), q_lr, k_lr, pole_rate, residue)
    return pl.pallas_call(
        hand_over,
        out_shape=(out, out),
        in_specs=[in_place] * 2,
        out_specs=(in_place, in_place),
        scratch_shapes=[
            pltpu.VMEM((2, tok, channels), BF16),
            pltpu.SemaphoreType.DMA((2, HAND_PIECES)),
            pltpu.SemaphoreType.DMA((2, HAND_PIECES)),
        ],
        compiler_params=pltpu.CompilerParams(vmem_limit_bytes=56 * 1024 * 1024),
        name="hand_over",
    )(*results)


def solution(mesh):
    placed = (
        P("ctx", "tp"),
        P("ctx", "tp"),
        P("ctx", "tp"),
        P("ctx", "tp"),
        P("tp", None),
        P("tp"),
        P("ctx", "tp"),
        P("ctx", "tp"),
        P(None, "tp"),
        P(None, "tp"),
    )
    return jax.shard_map(
        per_device,
        mesh=mesh,
        in_specs=placed,
        out_specs=(P("ctx", "tp"), P("ctx", "tp")),
        check_vma=False,
    )
```
